512 devices in a mesh: row: 16 (over y, x_lo, core), col: 16 (over z), rep: 2 (over x_hi).
Axes of the slice: x: 4 (x_hi: 2, x_lo: 2; x = x_hi * 2 + x_lo), y: 4, z: 16, core: 2. Of those that a mesh axis runs over, the one named last changes fastest.
Arguments:
- layer_inputs: bfloat16 [2, 2048, 6144], P('rep', 'col', 'row'), may hold values from -14 to 14
- output_grads: bfloat16 [2, 2048, 24576], P('rep', 'row', 'col'), may hold values from -0.30935922 to 0.30935922
- error_prev: bfloat16 [2, 6144, 24576], P('rep', 'row', 'col'), may hold values from -72 to 72
- basis_prev: bfloat16 [24576, 64], P('col'), may hold values from -6 to 6
Outputs:
- basis_next: float32 [24576, 64], P('col')
- error_next: bfloat16 [2, 6144, 24576], P('rep', 'row', 'col')
The draws below stay inside these ranges and needn't reach their ends.
All inputs are finite; a program needn't handle non-finite values.
Results may differ from the reference program's by a relative error of at most 0.005.
Values may be sent and summed in bfloat16 or wider, within the bound.
A program may use at most 64 MiB of HBM per device.

```python
import jax
import jax.numpy as jnp
from jax import lax

RANK = 64
TOKENS = 2048
N = 6144
M = 24576
REPS = 2


def ramp_scales(key, count, trend, rough):
    position = jnp.arange(count, dtype=jnp.float32) / count
    jitter = jax.random.uniform(key, (count,), jnp.float32, -rough, rough)
    return jnp.exp(trend * (position - 0.5) + jitter)


def base_values(key, shape):
    return jnp.clip(jax.random.normal(key, shape, jnp.float32), -4.0, 4.0)


def draw_layer_inputs(key, part):
    key = jax.random.fold_in(key, 11)
    first, second = jax.random.split(key)
    scales = ramp_scales(first, N, 1.0986, 0.6931)
    values = base_values(second, (REPS, TOKENS, N))
    return (values * scales[None, None, :]).astype(jnp.bfloat16)


def draw_output_grads(key, part):
    key = jax.random.fold_in(key, 23)
    first, second = jax.random.split(key)
    scales = ramp_scales(first, M, 1.0986, 0.6931)
    values = base_values(second, (REPS, TOKENS, M))
    return (values * scales[None, None, :] / TOKENS ** 0.5).astype(jnp.bfloat16)


def draw_error_prev(key, part):
    key = jax.random.fold_in(key, 37)
    first, second, third = jax.random.split(key, 3)
    row_scales = ramp_scales(first, N, 1.0986, 0.6931)
    col_scales = ramp_scales(second, M, 1.0986, 0.6931)
    values = base_values(third, (REPS, N, M))
    return (values * row_scales[None, :, None] * col_scales[None, None, :]).astype(jnp.bfloat16)


def shard_levels(key, shape, cuts, smallest, high):
    gain = 1.0
    for dim, shards_of in cuts:
        draws = jax.random.uniform(jax.random.fold_in(jax.random.fold_in(key, 6), dim), (shards_of,), jnp.float32, smallest / len(cuts), high / len(cuts))
        gain = gain * jnp.repeat(jnp.exp(draws), shape[dim] // shards_of).reshape((-1,) + (1,) * (len(shape) - 1 - dim))
    return gain


def noise(stream_key, dims, scale, reach, shards=(), held_as=jnp.bfloat16):
    loudness = shard_levels(stream_key, dims, shards, -0.22, 0.18) if shards else 1.0
    array = jax.random.normal(stream_key, dims, jnp.float32) * scale * loudness
    return jnp.minimum(jnp.maximum(array, -reach), reach).astype(held_as)


def setup_inputs(seed: int = 0) -> dict:
    splits = jax.random.split(jax.random.key(seed), 5)
    layer_inputs = draw_layer_inputs(jax.random.fold_in(splits[4], 71), 0)
    output_grads = draw_output_grads(jax.random.fold_in(splits[4], 71), 0)
    error_prev = draw_error_prev(jax.random.fold_in(splits[4], 71), 0)
    basis_prev = noise(splits[3], (M, RANK), 1.0, 6.0, ((0, 16),))
    return {"layer_inputs": layer_inputs, "output_grads": output_grads, "error_prev": error_prev, "basis_prev": basis_prev}


def reference(layer_inputs, output_grads, error_prev, basis_prev):
    pieces = []
    for index in range(REPS):
        gradient = lax.dot_general(layer_inputs[index].astype(jnp.float32), output_grads[index].astype(jnp.float32), (((0,), (0,)), ((), ())), preferred_element_type=jnp.float32)
        pieces.append((gradient + error_prev[index].astype(jnp.float32)).astype(jnp.bfloat16))
    projected = jnp.zeros((N, RANK), jnp.float32)
    for index in range(REPS):
        projected = projected + jnp.dot(pieces[index].astype(jnp.float32), basis_prev.astype(jnp.float32), preferred_element_type=jnp.float32)
    projected = projected / REPS
    gram_matrix = lax.dot_general(projected.astype(jnp.float32), projected.astype(jnp.float32), (((0,), (0,)), ((), ())), precision=lax.Precision.HIGHEST, preferred_element_type=jnp.float32)
    factor = jnp.linalg.cholesky(gram_matrix)
    ortho = lax.linalg.triangular_solve(factor, projected, left_side=False, lower=True, transpose_a=True)
    ortho_low = ortho.astype(jnp.bfloat16)
    basis_next = jnp.zeros((M, RANK), jnp.float32)
    for index in range(REPS):
        basis_next = basis_next + lax.dot_general(pieces[index].astype(jnp.float32), ortho_low.astype(jnp.float32), (((0,), (0,)), ((), ())), preferred_element_type=jnp.float32)
    basis_next = basis_next / REPS
    basis_low = basis_next.astype(jnp.bfloat16)
    approx = lax.dot_general(ortho_low.astype(jnp.float32), basis_low.astype(jnp.float32), (((1,), (1,)), ((), ())), preferred_element_type=jnp.float32)
    outputs = [(pieces[index].astype(jnp.float32) - approx).astype(jnp.bfloat16) for index in range(REPS)]
    return (basis_next, jnp.stack(outputs))
```

```python
import jax
import jax.numpy as jnp
from jax import lax
from jax.experimental import pallas as pl
from jax.experimental.pallas import tpu as pltpu
from jax.sharding import PartitionSpec as P

MESH = pl.DeviceIdType.MESH
HIGH = lax.Precision.HIGHEST
F32 = jnp.float32
BF16 = jnp.bfloat16

RING = 16
HALF = 64
RANK = 64


def dot(a, b, dims, precision=None):
    return lax.dot_general(a, b, (dims, ((), ())), precision=precision, preferred_element_type=F32)


def kernel(
    x_ref, g_ref, e_ref, b_ref,
    comp_ref, ortho_ref, basis_ref,
    xg, gg, acc, sf_out, sf_in, sf_own, sf_all, s_mine, s_all, p_mine, p_peer,
    gram_mine, gram_all, mat, u_out, u_in, u_own, u_all,
    loc_sem, xr_send, xr_recv, xl_send, xl_recv, g_send, g_recv, d_send, d_recv,
    sf_send, sf_recv, sa_send, sa_recv, s_send, s_recv, p_send, p_recv,
    gr_send, gr_recv, u_send, u_recv, ua_send, ua_recv,
):
    row, col, rep = lax.axis_index("row"), lax.axis_index("col"), lax.axis_index("rep")
    y, x, core = row // 4, (row // 2) % 2, row % 2

    def at_row(yy, xx, cc):
        return lax.rem(yy + 4, 4) * 4 + xx * 2 + cc

    def wrap(v):
        return lax.rem(v + RING, RING)

    def remote(src, dst, ssem, rsem, where):
        return pltpu.make_async_remote_copy(
            src_ref=src, dst_ref=dst, send_sem=ssem, recv_sem=rsem,
            device_id=where, device_id_type=MESH,
        )

    here = (row, col, 1 - rep)
    sends = []

    def send(src, dst, ssem, rsem, where):
        copy = remote(src, dst, ssem, rsem, where)
        copy.start()
        sends.append(copy)

    def arrived(dst, rsem):
        remote(dst, dst, rsem, rsem, here).wait_recv()

    barrier = pltpu.get_barrier_semaphore()

    def signal(where):
        pl.semaphore_signal(barrier, inc=1, device_id=where, device_id_type=MESH)

    @pl.loop(1, RING)
    def _(k):
        signal((row, wrap(col + k), rep))
        signal((wrap(row + k), col, rep))
        signal((wrap(row + k), col, 1 - rep))

    signal((row, col, 1 - rep))

    own_x = pltpu.make_async_copy(x_ref.at[0], xg.at[col], loc_sem.at[0])
    own_g = pltpu.make_async_copy(g_ref.at[0], gg.at[row], loc_sem.at[1])
    own_x.start()
    own_g.start()
    own_x.wait()
    own_g.wait()

    b_t = b_ref[...].T
    st = dot(b_t, gg[row], ((1,), (1,))).astype(BF16)
    ft = dot(b_t, e_ref[0], ((1,), (1,))).astype(BF16)
    for a in range(4):
        rows = slice(16 * a, 16 * a + 16)
        sf_out[4 * a] = st[rows, :]
        for b in range(3):
            sf_out[4 * a + b + 1] = ft[rows, 128 * b:128 * b + 128]

    pl.semaphore_wait(barrier, 3 * (RING - 1) + 1)

    @pl.loop(1, RING)
    def _(k):
        to = wrap(col + k)
        remote(sf_out.at[to], sf_in.at[col], sf_send, sf_recv, (row, to, rep)).start()

    sf_in[col] = sf_out[col]

    right, left = (row, wrap(col + 1), rep), (row, wrap(col - 1), rep)
    send(xg.at[col], xg.at[col], xr_send.at[0], xr_recv.at[0], right)
    send(xg.at[col], xg.at[col], xl_send.at[0], xl_recv.at[0], left)

    up, down, side, sib = (
        (at_row(y + 1, x, core), col, rep),
        (at_row(y - 1, x, core), col, rep),
        (at_row(y, 1 - x, core), col, rep),
        (at_row(y, x, 1 - core), col, rep),
    )
    XP, YM, YP, YMX, YPX, Y2A, Y2B, X2A, X2B, OWN = range(10)
    place = {
        OWN: (0, 0, None), XP: (0, 1, None), YM: (-1, 0, None), YP: (1, 0, None),
        YMX: (-1, 1, None), YPX: (1, 1, None), Y2A: (2, 0, 0), Y2B: (2, 0, 1),
        X2A: (2, 1, 0), X2B: (2, 1, 1),
    }

    def block(name, cc):
        dy, dx, half = place[name]
        slot = at_row(y + dy, x if dx == 0 else 1 - x, cc)
        return gg.at[slot] if half is None else gg.at[slot, pl.ds(half * HALF, HALF)]

    def push(src, k, dst, where):
        ref = block(src, core)
        if dst in (Y2A, Y2B):
            dy, dx, _ = place[src]
            half = 0 if dst == Y2A else 1
            ref = gg.at[at_row(y + dy, x, core), pl.ds(half * HALF, HALF)]
        send(ref, ref, g_send.at[k], g_recv.at[dst], where)

    def got(name):
        arrived(block(name, core), g_recv.at[name])
        share(name)

    def share(name):
        ref = block(name, core)
        send(ref, ref, d_send.at[name], d_recv.at[name], sib)

    def shared(name):
        arrived(block(name, 1 - core), d_recv.at[name])

    push(OWN, 0, XP, side)
    push(OWN, 1, YM, up)
    push(OWN, 2, YP, down)
    share(OWN)

    def x_step(s):
        frm, tol = wrap(col - s), wrap(col + s)
        if s < 8:
            arrived(xg.at[frm], xr_recv.at[s - 1])
            ref = xg.at[frm] if s < 7 else xg.at[frm, pl.ds(0, HALF)]
            send(ref, ref, xr_send.at[s], xr_recv.at[s], right)
            arrived(xg.at[tol], xl_recv.at[s - 1])
            ref = xg.at[tol] if s < 7 else xg.at[tol, pl.ds(HALF, HALF)]
            send(ref, ref, xl_send.at[s], xl_recv.at[s], left)
        else:
            arrived(xg.at[frm, pl.ds(0, HALF)], xr_recv.at[7])
            arrived(xg.at[tol, pl.ds(HALF, HALF)], xl_recv.at[7])

    x_step(1)

    def many(ref, sem):
        remote(ref, ref, sem, sem, here).wait_recv()

    def many_sent(ref, sem):
        remote(ref, ref, sem, sem, here).wait_send()

    many(sf_in.at[pl.ds(0, RING - 1)], sf_recv)
    sf_own[...] = jnp.sum(sf_in[...].astype(F32), axis=0).astype(BF16)

    @pl.loop(1, RING)
    def _(k):
        to = wrap(col + k)
        remote(sf_own, sf_all.at[col], sa_send, sa_recv, (row, to, rep)).start()

    sf_all[col] = sf_own[...]
    x_step(2)
    many(sf_all.at[pl.ds(0, RING - 1)], sa_recv)
    for a in range(4):
        s_mine[16 * a:16 * a + 16, :] = sf_all[4 * a]

    @pl.loop(1, RING)
    def _(k):
        to = wrap(row + k)
        remote(s_mine, s_all.at[row], s_send, s_recv, (to, col, rep)).start()

    s_all[row] = s_mine[...]
    x_step(3)
    got(YM)
    push(YM, 3, Y2A, up)
    got(YP)
    push(YP, 4, Y2B, down)
    got(XP)
    push(XP, 5, YMX, up)
    push(XP, 6, YPX, down)
    x_step(4)
    x_step(5)
    x_step(6)
    x_step(7)
    got(Y2A)
    push(Y2A, 7, X2A, side)
    got(Y2B)
    push(Y2B, 8, X2B, side)
    many(s_all.at[pl.ds(0, RING - 1)], s_recv)
    x_step(8)

    s_wide = jnp.concatenate([s_all[t] for t in range(RING)], axis=1)
    f_wide = jnp.concatenate(
        [jnp.concatenate([sf_all[4 * a + b + 1] for a in range(4)], axis=0) for b in range(3)],
        axis=1,
    )
    p_part = dot(s_wide, xg[...].reshape(RING * 128, 384), ((1,), (0,)))
    p_mine[...] = (p_part + f_wide.astype(F32)).astype(BF16)
    send(p_mine, p_peer, p_send, p_recv, (row, col, 1 - rep))

    def multiply(first, yy, xx):
        pair = lax.rem(yy + 4, 4) * 2 + xx
        xs = xg[pl.ds(2 * pair, 2)].reshape(256, 384)

        @pl.loop(0, 3)
        def _(n):
            cols = pl.ds(pl.multiple_of(n * 512, 512), 512)
            gs = gg[pl.ds(2 * pair, 2), :, cols].reshape(256, 512)
            if first:
                acc[:, cols] = e_ref[0, :, cols].astype(F32) + dot(xs, gs, ((0,), (0,)))
            else:
                acc[:, cols] += dot(xs, gs, ((0,), (0,)))

    shared(OWN)
    multiply(True, y, x)

    arrived(p_peer, p_recv)
    p_t = (p_mine[...].astype(F32) + p_peer[...].astype(F32)) * 0.5
    gram = dot(p_t, p_t, ((1,), (1,)), HIGH)
    gram_mine[...] = jnp.concatenate([gram[:32], gram[32:]], axis=1)

    @pl.loop(1, RING)
    def _(k):
        to = wrap(row + k)
        remote(gram_mine, gram_all.at[row], gr_send, gr_recv, (to, col, rep)).start()

    gram_all[row] = gram_mine[...]

    shared(XP)
    multiply(False, y, 1 - x)
    shared(YM)
    multiply(False, y - 1, x)
    shared(YP)
    multiply(False, y + 1, x)

    many(gram_all.at[pl.ds(0, RING - 1)], gr_recv)
    total = jnp.sum(gram_all[...], axis=0)
    gram = jnp.concatenate([total[:, :RANK], total[:, RANK:]], axis=0)
    subl = lax.broadcasted_iota(jnp.int32, (RANK, 128), 0)
    lane = lax.broadcasted_iota(jnp.int32, (RANK, 128), 1)
    mat[...] = jnp.concatenate([gram, (subl == lane)[:, :RANK].astype(F32)], axis=1)

    def eliminate(k, carry):
        m = mat[...]
        pivot_row = mat[pl.ds(k, 1), :]
        column = jnp.sum(jnp.where(lane == k, m, 0.0), axis=1, keepdims=True)
        pivot = jnp.sum(jnp.where(lane[:1] == k, pivot_row, 0.0), axis=1, keepdims=True)
        factor = jnp.where(subl[:, :1] > k, column / pivot, 0.0)
        mat[...] = m - factor * pivot_row
        return carry

    lax.fori_loop(0, RANK, eliminate, 0)

    got(YMX)
    got(YPX)
    shared(Y2A)
    shared(Y2B)
    multiply(False, y + 2, x)
    shared(YMX)
    multiply(False, y - 1, 1 - x)
    shared(YPX)
    multiply(False, y + 1, 1 - x)
    got(X2A)
    got(X2B)
    shared(X2A)
    shared(X2B)
    multiply(False, y + 2, 1 - x)

    comp_ref[...] = acc[...].astype(BF16)

    p_low = p_t.astype(BF16)
    for b in range(4):
        cols = slice(384 * b, 384 * b + 384)
        ut = dot(p_low, comp_ref[:, cols], ((1,), (0,))).astype(BF16)
        for a in range(4):
            u_out[4 * a + b] = ut[16 * a:16 * a + 16, :]

    me = row + RING * rep
    mine = row // 2 + 8 * rep
    owner = core == x

    def piece_at(k):
        chip = lax.rem(k, 8)
        return (2 * chip + lax.rem(chip, 2), col, k // 8)

    @pl.loop(0, RING)
    def _(k):
        @pl.when(jnp.logical_not(jnp.logical_and(owner, k == mine)))
        def _():
            remote(u_out.at[k], u_in.at[me], u_send, u_recv, piece_at(k)).start()

    d = jnp.sum(jnp.where(lane == subl, mat[...], 0.0), axis=1, keepdims=True)
    inv_factor = lax.rsqrt(d) * mat[:, RANK:]

    ortho_ref[...] = dot(inv_factor, p_t, ((1,), (0,)), HIGH).astype(BF16)

    @pl.when(owner)
    def _():
        u_in[me] = u_out[mine]
        many(u_in.at[pl.ds(0, 31)], u_recv)
        u_own[...] = jnp.sum(u_in[...].astype(F32), axis=0).astype(BF16)

        @pl.loop(1, 32)
        def _(k):
            to = lax.rem(me + k, 32)
            remote(u_own, u_all.at[mine], ua_send, ua_recv, (lax.rem(to, RING), col, to // RING)).start()

        u_all[mine] = u_own[...]
        many(u_all.at[pl.ds(0, 15)], ua_recv)
        many_sent(u_out.at[pl.ds(0, 15)], u_send)
        many_sent(u_in.at[pl.ds(0, 31)], ua_send)

    @pl.when(jnp.logical_not(owner))
    def _():
        many(u_all, ua_recv)
        many_sent(u_out, u_send)

    for b in range(4):
        ut = jnp.concatenate([u_all[4 * a + b] for a in range(4)], axis=0).astype(F32) * 0.5
        basis_ref[:, 384 * b:384 * b + 384] = dot(inv_factor, ut, ((1,), (0,)), HIGH)

    for copy in sends:
        copy.wait_send()
    many_sent(sf_out.at[pl.ds(0, 15)], sf_send)
    many_sent(sf_in.at[pl.ds(0, 15)], sa_send)
    many_sent(s_all.at[pl.ds(0, 15)], s_send)
    many_sent(gram_all.at[pl.ds(0, 15)], gr_send)


def body(layer_inputs, output_grads, error_prev, basis_prev):
    dma = pltpu.SemaphoreType.DMA
    comp, ortho_t, basis_t = pl.pallas_call(
        kernel,
        out_shape=(
            jax.ShapeDtypeStruct((384, 1536), BF16),
            jax.ShapeDtypeStruct((RANK, 384), BF16),
            jax.ShapeDtypeStruct((RANK, 1536), F32),
        ),
        in_specs=[
            pl.BlockSpec(memory_space=pl.ANY),
            pl.BlockSpec(memory_space=pl.ANY),
            pl.BlockSpec(memory_space=pltpu.VMEM),
            pl.BlockSpec(memory_space=pltpu.VMEM),
        ],
        out_specs=[pl.BlockSpec(memory_space=pltpu.VMEM)] * 3,
        scratch_shapes=[
            pltpu.VMEM((16, 128, 384), BF16),
            pltpu.VMEM((16, 128, 1536), BF16),
            pltpu.VMEM((384, 1536), F32),
            pltpu.VMEM((16, 16, 128), BF16),
            pltpu.VMEM((16, 16, 128), BF16),
            pltpu.VMEM((16, 128), BF16),
            pltpu.VMEM((16, 16, 128), BF16),
            pltpu.VMEM((64, 128), BF16),
            pltpu.VMEM((16, 64, 128), BF16),
            pltpu.VMEM((64, 384), BF16),
            pltpu.VMEM((64, 384), BF16),
            pltpu.VMEM((32, 128), F32),
            pltpu.VMEM((16, 32, 128), F32),
            pltpu.VMEM((64, 128), F32),
            pltpu.VMEM((16, 16, 384), BF16),
            pltpu.VMEM((32, 16, 384), BF16),
            pltpu.VMEM((16, 384), BF16),
            pltpu.VMEM((16, 16, 384), BF16),
            dma((2,)),
            dma((8,)), dma((8,)), dma((8,)), dma((8,)),
            dma((9,)), dma((9,)), dma((10,)), dma((10,)),
        ] + [dma(())] * 14,
        compiler_params=pltpu.CompilerParams(
            collective_id=0, has_side_effects=True, vmem_limit_bytes=48 * 2**20
        ),
        name="powersgd",
    )(layer_inputs, output_grads, error_prev, basis_prev)
    basis_next = basis_t.T
    approx = dot(ortho_t, basis_t.astype(BF16), ((0,), (0,)))
    error_next = (comp.astype(F32) - approx).astype(BF16)
    return (basis_next, error_next[None])


def solution(mesh):
    return jax.shard_map(
        body,
        mesh=mesh,
        in_specs=(
            P("rep", "col", "row"),
            P("rep", "row", "col"),
            P("rep", "row", "col"),
            P("col", None),
        ),
        out_specs=(P("col", None), P("rep", "row", "col")),
        check_vma=False,
    )
```

```python
import jax
import jax.numpy as jnp
from jax import lax
from jax.experimental import pallas as pl
from jax.experimental.pallas import tpu as pltpu
from jax.sharding import PartitionSpec as P

MESH = pl.DeviceIdType.MESH
HIGH = lax.Precision.HIGHEST
F32 = jnp.float32
BF16 = jnp.bfloat16

RING = 16
HALF = 64
RANK = 64


def dot(a, b, dims, precision=None):
    return lax.dot_general(a, b, (dims, ((), ())), precision=precision, preferred_element_type=F32)


def kernel(
    x_ref, g_ref, e_ref, bt_ref,
    comp_ref, ortho_ref, basis_ref,
    xg, gg, acc, xt, e_in, bt, s_one, s_two, f_out, f_in, f_own, f_all, s_all, p_mine, p_peer,
    gram_mine, gram_all, mat, u_out, u_in, u_own, u_all,
    loc_sem, x_send, xr_recv, xl_recv, g_send, g_recv, d_send, d_recv,
    s_send, s_recv, f_send, f_recv, r_send, r_recv, p_send, p_recv, gr_send, gr_recv, u_send, u_recv, near,
):
    row, col, rep = lax.axis_index("row"), lax.axis_index("col"), lax.axis_index("rep")
    y, x, core = row // 4, (row // 2) % 2, row % 2

    def at_row(yy, xx, cc):
        return lax.rem(yy + 4, 4) * 4 + xx * 2 + cc

    def wrap(v):
        return lax.rem(v + RING, RING)

    def remote(src, dst, ssem, rsem, where):
        return pltpu.make_async_remote_copy(
            src_ref=src, dst_ref=dst, send_sem=ssem, recv_sem=rsem,
            device_id=where, device_id_type=MESH,
        )

    here = (row, col, 1 - rep)
    sends = []

    def send(src, dst, ssem, rsem, where):
        copy = remote(src, dst, ssem, rsem, where)
        copy.start()
        sends.append(copy)

    def arrived(dst, rsem):
        remote(dst, dst, rsem, rsem, here).wait_recv()

    def sent(src, ssem):
        remote(src, src, ssem, ssem, here).wait_send()

    own_g = pltpu.make_async_copy(g_ref.at[0], gg.at[row], loc_sem.at[0])
    own_b = pltpu.make_async_copy(bt_ref, bt, loc_sem.at[1])
    own_x = pltpu.make_async_copy(x_ref.at[0], xg.at[col], loc_sem.at[2])
    own_e = pltpu.make_async_copy(e_ref.at[0], e_in, loc_sem.at[3])
    for copy in (own_g, own_b, own_x, own_e):
        copy.start()

    barrier = pltpu.get_barrier_semaphore()

    def signal(where):
        pl.semaphore_signal(barrier, inc=1, device_id=where, device_id_type=MESH)

    right, left = (row, wrap(col + 1), rep), (row, wrap(col - 1), rep)
    up, down, side, sib = (
        (at_row(y + 1, x, core), col, rep),
        (at_row(y - 1, x, core), col, rep),
        (at_row(y, 1 - x, core), col, rep),
        (at_row(y, x, 1 - core), col, rep),
    )
    for where in (right, left, up, down, side, sib, here):
        signal(where)

    def tell(k, *to):
        for where in to:
            pl.semaphore_signal(near.at[k], inc=1, device_id=where, device_id_type=MESH)

    def told(k, count):
        pl.semaphore_wait(near.at[k], count)

    own_g.wait()
    own_b.wait()
    quarter, group = lax.rem(col, 4), col // 4
    s_one[quarter] = dot(bt[...], gg[row], ((1,), (1,))).astype(BF16)
    own_x.wait()

    pl.semaphore_wait(barrier, 7)
    plane = (up, down, side, sib)

    def x_half(owner, half):
        return xg.at[owner, pl.ds(half * HALF, HALF)]

    def x_push(owner, half, k, side):
        ref = x_half(owner, half)
        recv = (xr_recv if side == 0 else xl_recv).at[2 * k + half]
        send(ref, ref, x_send.at[side, 2 * k + half], recv, right if side == 0 else left)

    for half in range(2):
        x_push(col, half, 0, 0)
        x_push(col, 1 - half, 0, 1)

    def x_step(k):
        frm, to = wrap(col - k), wrap(col + k)
        for i in range(2):
            half = i
            if k < 8 or half == 0:
                arrived(x_half(frm, half), xr_recv.at[2 * k - 2 + half])
                if k < 7 or (k == 7 and half == 0):
                    x_push(frm, half, k, 0)
            half = 1 - i
            if k < 8 or half == 1:
                arrived(x_half(to, half), xl_recv.at[2 * k - 2 + half])
                if k < 7 or (k == 7 and half == 1):
                    x_push(to, half, k, 1)

    XP, YM, YP, YMX, YPX, Y2A, Y2B, X2A, X2B, OWN = range(10)
    place = {
        OWN: (0, 0, None), XP: (0, 1, None), YM: (-1, 0, None), YP: (1, 0, None),
        YMX: (-1, 1, None), YPX: (1, 1, None), Y2A: (2, 0, 0), Y2B: (2, 0, 1),
        X2A: (2, 1, 0), X2B: (2, 1, 1),
    }

    def block(name, cc):
        dy, dx, half = place[name]
        slot = at_row(y + dy, x if dx == 0 else 1 - x, cc)
        return gg.at[slot] if half is None else gg.at[slot, pl.ds(half * HALF, HALF)]

    def push(src, k, dst, where):
        ref = block(src, core)
        if dst in (Y2A, Y2B):
            dy, dx, _ = place[src]
            half = 0 if dst == Y2A else 1
            ref = gg.at[at_row(y + dy, x, core), pl.ds(half * HALF, HALF)]
        send(ref, ref, g_send.at[k], g_recv.at[dst], where)

    def got(name):
        arrived(block(name, core), g_recv.at[name])
        share(name)

    def share(name):
        ref = block(name, core)
        send(ref, ref, d_send.at[name], d_recv.at[name], sib)

    def shared(name):
        arrived(block(name, 1 - core), d_recv.at[name])

    push(OWN, 0, XP, side)
    push(OWN, 1, YM, up)
    push(OWN, 2, YP, down)
    share(OWN)
    tell(0, right, left)
    tell(3, *plane)

    own_e.wait()
    ft = dot(bt[...], e_in[...], ((1,), (1,))).astype(BF16)
    for a in range(4):
        for b in range(3):
            f_out[4 * a + b + 1] = ft[16 * a:16 * a + 16, 128 * b:128 * b + 128]
    f_owner = quarter > 0
    f_count = 12

    told(0, 2)
    tell(1, (row, wrap(col + 2), rep), (row, wrap(col - 2), rep))
    told(3, 4)
    tell(4, *plane)
    told(1, 2)
    tell(2, (row, wrap(col + 4), rep), (row, wrap(col - 4), rep))

    for k in range(1, 4):
        to = lax.rem(quarter + k, 4)
        send(s_one.at[quarter], s_one.at[quarter], s_send.at[0, k], s_recv.at[0, k], (row, group * 4 + to, rep))

    x_step(1)
    told(4, 4)
    tell(5, *plane)
    told(2, 2)

    @pl.loop(1, RING)
    def _(k):
        to = wrap(col + k)

        @pl.when(lax.rem(to, 4) > 0)
        def _():
            remote(f_out.at[to], f_in.at[col], f_send.at[0], f_recv.at[0], (row, to, rep)).start()

    x_step(2)
    for k in range(1, 4):
        arrived(s_one.at[lax.rem(quarter + 4 - k, 4)], s_recv.at[0, k])
    s_two[group] = jnp.sum(s_one[...].astype(F32), axis=0).astype(BF16)
    for k in range(1, 4):
        to = lax.rem(group + k, 4)
        send(s_two.at[group], s_two.at[group], s_send.at[1, k], s_recv.at[1, k], (row, to * 4 + quarter, rep))
    told(5, 4)
    tell(6, here)
    x_step(3)
    got(YM)
    push(YM, 3, Y2A, up)
    got(YP)
    push(YP, 4, Y2B, down)
    got(XP)
    push(XP, 5, YMX, up)
    push(XP, 6, YPX, down)
    x_step(4)

    @pl.when(f_owner)
    def _():
        f_in[col] = f_out[col]
        arrived(f_in.at[pl.ds(0, RING - 1)], f_recv.at[0])
        f_own[...] = jnp.sum(f_in[...].astype(F32), axis=0).astype(BF16)

        @pl.loop(1, RING)
        def _(k):
            remote(f_own, f_all.at[col], f_send.at[1], f_recv.at[1], (row, wrap(col + k), rep)).start()

        f_all[col] = f_own[...]
        sent(f_out.at[pl.ds(0, f_count - 1)], f_send.at[0])
        sent(f_in.at[pl.ds(0, RING - 1)], f_send.at[1])

    for k in range(1, 4):
        arrived(s_two.at[lax.rem(group + 4 - k, 4)], s_recv.at[1, k])
    s_all[row] = jnp.sum(s_two[...].astype(F32), axis=0).astype(BF16)

    @pl.loop(1, RING)
    def _(k):
        remote(s_all.at[row], s_all.at[row], r_send.at[0], r_recv.at[0], (wrap(row + k), col, rep)).start()

    x_step(5)
    got(Y2A)
    push(Y2A, 7, X2A, side)
    got(Y2B)
    push(Y2B, 8, X2B, side)
    x_step(6)

    @pl.when(f_owner)
    def _():
        arrived(f_all.at[pl.ds(0, f_count - 1)], f_recv.at[1])

    @pl.when(jnp.logical_not(f_owner))
    def _():
        arrived(f_all.at[pl.ds(0, f_count)], f_recv.at[1])
        sent(f_out.at[pl.ds(0, f_count)], f_send.at[0])

    x_step(7)
    arrived(s_all.at[pl.ds(0, RING - 1)], r_recv.at[0])
    x_step(8)

    s_wide = jnp.concatenate([s_all[t] for t in range(RING)], axis=1)
    f_wide = jnp.concatenate(
        [jnp.concatenate([f_all[4 * a + b + 1] for a in range(4)], axis=0) for b in range(3)],
        axis=1,
    )
    p_part = dot(s_wide, xg[...].reshape(RING * 128, 384), ((1,), (0,)))
    p_mine[...] = p_part + f_wide.astype(F32)
    send(p_mine, p_peer, p_send, p_recv, (row, col, 1 - rep))

    def multiply(first, yy, xx):
        pair = lax.rem(yy + 4, 4) * 2 + xx
        xt[...] = xg[pl.ds(2 * pair, 2)].reshape(256, 384).T

        @pl.loop(0, 3)
        def _(n):
            cols = pl.ds(pl.multiple_of(n * 512, 512), 512)
            gs = gg[pl.ds(2 * pair, 2), :, cols].reshape(256, 512)
            if first:
                acc[:, cols] = e_in[:, cols].astype(F32) + dot(xt[...], gs, ((1,), (0,)))
            else:
                acc[:, cols] += dot(xt[...], gs, ((1,), (0,)))

    shared(OWN)
    multiply(True, y, x)
    shared(XP)
    multiply(False, y, 1 - x)
    shared(YM)
    multiply(False, y - 1, x)
    shared(YP)
    multiply(False, y + 1, x)
    got(YMX)
    got(YPX)
    shared(Y2A)
    shared(Y2B)
    multiply(False, y + 2, x)
    shared(YMX)
    multiply(False, y - 1, 1 - x)
    shared(YPX)
    multiply(False, y + 1, 1 - x)
    got(X2A)
    got(X2B)
    shared(X2A)
    shared(X2B)
    multiply(False, y + 2, 1 - x)
    comp_ref[...] = acc[...].astype(BF16)

    told(6, 1)
    arrived(p_peer, p_recv)
    p_t = (p_mine[...] + p_peer[...]) * 0.5

    p_high = p_t.astype(BF16)
    p_rest = (p_t - p_high.astype(F32)).astype(BF16)
    p_both = jnp.concatenate([p_high, p_rest], axis=0)
    me = row + RING * rep
    mine = row // 2 + 8 * rep
    owner = core == x

    def piece_at(k):
        chip = lax.rem(k, 8)
        return (2 * chip + lax.rem(chip, 2), col, k // 8)

    for b in range(4):
        cols = slice(384 * b, 384 * b + 384)
        ut = dot(p_both, comp_ref[:, cols], ((1,), (0,)))
        ut = (ut[:RANK] + ut[RANK:]).astype(BF16)
        for a in range(4):
            u_out[4 * a + b] = ut[16 * a:16 * a + 16, :]

    @pl.loop(0, RING)
    def _(k):
        @pl.when(jnp.logical_not(jnp.logical_and(owner, k == mine)))
        def _():
            remote(u_out.at[k], u_in.at[me], u_send.at[0], u_recv.at[0], piece_at(k)).start()

    gram = dot(p_t, p_t, ((1,), (1,)), HIGH)
    gram_mine[...] = jnp.concatenate([gram[:32], gram[32:]], axis=1)

    @pl.loop(1, RING)
    def _(k):
        to = wrap(row + k)
        remote(gram_mine, gram_all.at[row], gr_send, gr_recv, (to, col, rep)).start()

    gram_all[row] = gram_mine[...]

    @pl.when(owner)
    def _():
        u_in[me] = u_out[mine]
        arrived(u_in.at[pl.ds(0, 31)], u_recv.at[0])
        u_own[...] = jnp.sum(u_in[...].astype(F32), axis=0).astype(BF16)

        @pl.loop(1, 32)
        def _(k):
            to = lax.rem(me + k, 32)
            remote(u_own, u_all.at[mine], u_send.at[1], u_recv.at[1], (lax.rem(to, RING), col, to // RING)).start()

        u_all[mine] = u_own[...]

    arrived(gram_all.at[pl.ds(0, RING - 1)], gr_recv)
    total = jnp.sum(gram_all[...], axis=0)
    gram = jnp.concatenate([total[:, :RANK], total[:, RANK:]], axis=0)
    subl = lax.broadcasted_iota(jnp.int32, (RANK, 128), 0)
    lane = lax.broadcasted_iota(jnp.int32, (RANK, 128), 1)
    mat[...] = jnp.concatenate([gram, (subl == lane)[:, :RANK].astype(F32)], axis=1)

    def eliminate(k, carry):
        m = mat[...]
        pivot_row = mat[pl.ds(k, 1), :]
        column = jnp.sum(jnp.where(lane == k, m, 0.0), axis=1, keepdims=True)
        pivot = jnp.sum(jnp.where(lane[:1] == k, pivot_row, 0.0), axis=1, keepdims=True)
        factor = jnp.where(subl[:, :1] > k, column / pivot, 0.0)
        mat[...] = m - factor * pivot_row
        return carry

    lax.fori_loop(0, RANK, eliminate, 0)
    d = jnp.sum(jnp.where(lane == subl, mat[...], 0.0), axis=1, keepdims=True)
    inv_factor = lax.rsqrt(d) * mat[:, RANK:]
    ortho_ref[...] = dot(inv_factor, p_t, ((1,), (0,)), HIGH).astype(BF16)

    @pl.when(owner)
    def _():
        arrived(u_all.at[pl.ds(0, 15)], u_recv.at[1])
        sent(u_out.at[pl.ds(0, 15)], u_send.at[0])
        sent(u_in.at[pl.ds(0, 31)], u_send.at[1])

    @pl.when(jnp.logical_not(owner))
    def _():
        arrived(u_all, u_recv.at[1])
        sent(u_out, u_send.at[0])

    for b in range(4):
        ut = jnp.concatenate([u_all[4 * a + b] for a in range(4)], axis=0).astype(F32) * 0.5
        basis_ref[:, 384 * b:384 * b + 384] = dot(inv_factor, ut, ((1,), (0,)), HIGH)

    for copy in sends:
        copy.wait_send()
    sent(s_all.at[pl.ds(0, 15)], r_send.at[0])
    sent(gram_all.at[pl.ds(0, 15)], gr_send)


def body(layer_inputs, output_grads, error_prev, basis_prev):
    dma = pltpu.SemaphoreType.DMA
    vmem = pltpu.VMEM
    comp, ortho_t, basis_t = pl.pallas_call(
        kernel,
        out_shape=(
            jax.ShapeDtypeStruct((384, 1536), BF16),
            jax.ShapeDtypeStruct((RANK, 384), BF16),
            jax.ShapeDtypeStruct((RANK, 1536), F32),
        ),
        in_specs=[pl.BlockSpec(memory_space=pl.ANY)] * 4,
        out_specs=[pl.BlockSpec(memory_space=vmem)] * 3,
        scratch_shapes=[
            vmem((16, 128, 384), BF16),
            vmem((16, 128, 1536), BF16),
            vmem((384, 1536), F32),
            vmem((384, 256), BF16),
            vmem((384, 1536), BF16),
            vmem((RANK, 1536), BF16),
            vmem((4, RANK, 128), BF16),
            vmem((4, RANK, 128), BF16),
            vmem((16, 16, 128), BF16),
            vmem((16, 16, 128), BF16),
            vmem((16, 128), BF16),
            vmem((16, 16, 128), BF16),
            vmem((16, RANK, 128), BF16),
            vmem((RANK, 384), F32),
            vmem((RANK, 384), F32),
            vmem((32, 128), F32),
            vmem((16, 32, 128), F32),
            vmem((RANK, 128), F32),
            vmem((16, 16, 384), BF16),
            vmem((32, 16, 384), BF16),
            vmem((16, 384), BF16),
            vmem((16, 16, 384), BF16),
            dma((4,)),
            dma((2, 16)), dma((16,)), dma((16,)),
            dma((9,)), dma((9,)), dma((10,)), dma((10,)),
            dma((2, 4)), dma((2, 4)), dma((2,)), dma((2,)), dma((1,)), dma((1,)),
            dma(()), dma(()), dma(()), dma(()), dma((2,)), dma((2,)),
            pltpu.SemaphoreType.REGULAR((7,)),
        ],
        compiler_params=pltpu.CompilerParams(
            collective_id=0, has_side_effects=True, vmem_limit_bytes=60 * 2**20
        ),
        name="powersgd",
    )(layer_inputs, output_grads, error_prev, basis_prev.T)
    basis_next = basis_t.T
    approx = dot(ortho_t, basis_t.astype(BF16), ((0,), (0,)))
    error_next = (comp.astype(F32) - approx).astype(BF16)
    return (basis_next, error_next[None])


def solution(mesh):
    return jax.shard_map(
        body,
        mesh=mesh,
        in_specs=(
            P("rep", "col", "row"),
            P("rep", "row", "col"),
            P("rep", "row", "col"),
            P("col", None),
        ),
        out_specs=(P("col", None), P("rep", "row", "col")),
        check_vma=False,
    )
```

```python
import functools

import jax
import jax.numpy as jnp
from jax import lax
from jax.experimental import pallas as pl
from jax.experimental.pallas import tpu as pltpu
from jax.sharding import PartitionSpec as P

MESH = pl.DeviceIdType.MESH
HIGH = lax.Precision.HIGHEST
F32 = jnp.float32
BF16 = jnp.bfloat16

RING = 16
HALF = 64
RANK = 64
PARTS = 4
ROWS = 128 // PARTS


ORDER = (
    "s_near start_x start_g t_zero f_make t_one x1 t_three s_far x2 f_send_out t_four x3 "
    "g_ym g_yp g_xp p_xp x4 f_sum s_row x5 g_y2 x6 f_end x7 s_end x8 g_rest p_make "
    "g_last c_one c_two t_five c_three c_four"
)


def dot(a, b, dims, precision=None):
    return lax.dot_general(a, b, (dims, ((), ())), precision=precision, preferred_element_type=F32)


def kernel(
    x_ref, g_ref, e_ref, bt_ref,
    comp_hbm, ortho_ref, basis_ref,
    xg, gg, acc, xt, comp_ref, e_in, bt, s_one, s_two, f_out, f_in, f_own, f_all, s_all, p_mine, p_peer,
    gram_mine, gram_all, mat, u_out, u_in, u_own, u_all,
    loc_sem, x_send, xr_recv, xl_recv, g_send, g_recv, d_send, d_recv,
    s_send, s_recv, f_send, f_recv, r_send, r_recv, p_send, p_recv, gr_send, gr_recv, u_send, u_recv, near,
):
    row, col, rep = lax.axis_index("row"), lax.axis_index("col"), lax.axis_index("rep")
    y, x, core = row // 4, (row // 2) % 2, row % 2

    def at_row(yy, xx, cc):
        return lax.rem(yy + 4, 4) * 4 + xx * 2 + cc

    def wrap(v):
        return lax.rem(v + RING, RING)

    def place_of(dy, dx):
        return dy + dy // 2 - 2 * (dy // 3) + 4 * dx

    def remote(src, dst, ssem, rsem, where):
        return pltpu.make_async_remote_copy(
            src_ref=src, dst_ref=dst, send_sem=ssem, recv_sem=rsem,
            device_id=where, device_id_type=MESH,
        )

    here = (row, col, 1 - rep)
    sends = []

    def send(src, dst, ssem, rsem, where):
        copy = remote(src, dst, ssem, rsem, where)
        copy.start()
        sends.append(copy)

    def arrived(dst, rsem):
        remote(dst, dst, rsem, rsem, here).wait_recv()

    def sent(src, ssem):
        remote(src, src, ssem, ssem, here).wait_send()

    own_g = pltpu.make_async_copy(g_ref, gg.at[pl.ds(0, 2)], loc_sem.at[0])
    own_b = pltpu.make_async_copy(bt_ref, bt, loc_sem.at[1])
    own_x = pltpu.make_async_copy(x_ref, xg.at[pl.ds(PARTS * col, PARTS)], loc_sem.at[2])
    own_e = pltpu.make_async_copy(e_ref.at[0], e_in, loc_sem.at[3])
    for copy in (own_g, own_b, own_x, own_e):
        copy.start()

    barrier = pltpu.get_barrier_semaphore()

    def signal(where):
        pl.semaphore_signal(barrier, inc=1, device_id=where, device_id_type=MESH)

    right, left = (row, wrap(col + 1), rep), (row, wrap(col - 1), rep)
    up, down, side, sib = (
        (at_row(y + 1, x, core), col, rep),
        (at_row(y - 1, x, core), col, rep),
        (at_row(y, 1 - x, core), col, rep),
        (at_row(y, x, 1 - core), col, rep),
    )
    for where in (right, left, up, down, side, sib, here):
        signal(where)
    for k in (2, 3):
        signal((row, wrap(col + k), rep))
        signal((row, wrap(col - k), rep))

    def tell(k, *to):
        for where in to:
            pl.semaphore_signal(near.at[k], inc=1, device_id=where, device_id_type=MESH)

    def told(k, count):
        pl.semaphore_wait(near.at[k], count)

    own_g.wait()
    own_b.wait()
    quarter, group = lax.rem(col, 4), col // 4
    s_one[quarter] = dot(bt[...], gg[0:2].reshape(128, 1536), ((1,), (1,))).astype(BF16)
    own_x.wait()

    pl.semaphore_wait(barrier, 11)
    plane = (up, down, side, sib)

    def x_part(owner, part):
        return xg.at[PARTS * owner + part]

    def x_push(owner, part, k, side):
        ref = x_part(owner, part)
        recv = (xr_recv if side == 0 else xl_recv).at[PARTS * k + part]
        remote(ref, ref, x_send.at[side], recv, right if side == 0 else left).start()

    def x_turn(owner):
        slot = 2 * place_of(lax.rem(owner // 4 - y + 4, 4), lax.rem(owner // 2 + x, 2)) + lax.rem(owner + core, 2)
        xt[:, pl.ds(pl.multiple_of(slot * 128, 128), 128)] = xg[pl.ds(PARTS * owner, PARTS)].reshape(128, 384).T

    def x_step(k):
        frm, to = wrap(col - k), wrap(col + k)
        for i in range(PARTS):
            if k < 8 or i < PARTS // 2:
                arrived(x_part(frm, i), xr_recv.at[PARTS * (k - 1) + i])
                if k < 7 or (k == 7 and i < PARTS // 2):
                    x_push(frm, i, k, 0)
            i = PARTS - 1 - i
            if k < 8 or i >= PARTS // 2:
                arrived(x_part(to, i), xl_recv.at[PARTS * (k - 1) + i])
                if k < 7 or (k == 7 and i >= PARTS // 2):
                    x_push(to, i, k, 1)
        x_turn(frm)
        if k < 8:
            x_turn(to)

    OWN, YP, YM, Y2, XP, YPX, YMX, Y2X = range(8)
    FIRST, SECOND, WHOLE = (0, 1), (1, 1), (0, 2)

    def block(name, part, other=0):
        return gg.at[pl.ds(2 * (2 * name + other) + part[0], part[1])]

    def push(src, k, dst, where, part=WHOLE):
        remote(block(src, part), block(dst, part), g_send, g_recv.at[k], where).start()

    def got(k, name, part=WHOLE):
        arrived(block(name, part), g_recv.at[k])
        share(k, name, part)

    def share(k, name, part=WHOLE):
        remote(block(name, part), block(name, part, 1), d_send, d_recv.at[k], sib).start()

    def shared(k, name, part=WHOLE):
        arrived(block(name, part, 1), d_recv.at[k])

    def start_x():
        for part in range(PARTS):
            x_push(col, part, 0, 0)
            x_push(col, PARTS - 1 - part, 0, 1)
        x_turn(col)

    def start_g():
        push(OWN, 0, XP, side)
        push(OWN, 1, YM, up)
        push(OWN, 2, YP, down)
        share(9, OWN)

    def g_ym():
        got(1, YM)
        push(YM, 3, Y2, up, FIRST)

    def g_yp():
        got(2, YP)
        push(YP, 4, Y2, down, SECOND)

    def g_xp():
        got(0, XP)

    def p_xp():
        push(XP, 5, YMX, up)
        push(XP, 6, YPX, down)

    def g_y2():
        got(3, Y2, FIRST)
        push(Y2, 7, Y2X, side, FIRST)
        got(4, Y2, SECOND)
        push(Y2, 8, Y2X, side, SECOND)

    f_owner = quarter > 0
    f_count = 12

    def f_make():
        own_e.wait()
        ft = dot(bt[...], e_in[...], ((1,), (1,))).astype(BF16)
        for a in range(4):
            for b in range(3):
                f_out[4 * a + b + 1] = ft[16 * a:16 * a + 16, 128 * b:128 * b + 128]

    def f_send_out():
        @pl.loop(1, RING)
        def _(k):
            to = wrap(col + k)

            @pl.when(lax.rem(to, 4) > 0)
            def _():
                remote(f_out.at[to], f_in.at[col], f_send.at[0], f_recv.at[0], (row, to, rep)).start()

    def f_sum():
        @pl.when(f_owner)
        def _():
            f_in[col] = f_out[col]
            arrived(f_in.at[pl.ds(0, RING - 1)], f_recv.at[0])
            f_own[...] = jnp.sum(f_in[...].astype(F32), axis=0).astype(BF16)

            @pl.loop(1, RING)
            def _(k):
                remote(f_own, f_all.at[col], f_send.at[1], f_recv.at[1], (row, wrap(col + k), rep)).start()

            f_all[col] = f_own[...]
            sent(f_out.at[pl.ds(0, f_count - 1)], f_send.at[0])

    def f_end():
        @pl.when(f_owner)
        def _():
            arrived(f_all.at[pl.ds(0, f_count - 1)], f_recv.at[1])
            sent(f_in.at[pl.ds(0, RING - 1)], f_send.at[1])

        @pl.when(jnp.logical_not(f_owner))
        def _():
            arrived(f_all.at[pl.ds(0, f_count)], f_recv.at[1])
            sent(f_out.at[pl.ds(0, f_count)], f_send.at[0])

    def s_near():
        for k in range(1, 4):
            to = lax.rem(quarter + k, 4)
            send(s_one.at[quarter], s_one.at[quarter], s_send.at[0, k], s_recv.at[0, k], (row, group * 4 + to, rep))

    def s_far():
        for k in range(1, 4):
            arrived(s_one.at[lax.rem(quarter + 4 - k, 4)], s_recv.at[0, k])
        s_two[group] = jnp.sum(s_one[...].astype(F32), axis=0).astype(BF16)
        for k in range(1, 4):
            to = lax.rem(group + k, 4)
            send(s_two.at[group], s_two.at[group], s_send.at[1, k], s_recv.at[1, k], (row, to * 4 + quarter, rep))

    def s_row():
        for k in range(1, 4):
            arrived(s_two.at[lax.rem(group + 4 - k, 4)], s_recv.at[1, k])
        s_all[row] = jnp.sum(s_two[...].astype(F32), axis=0).astype(BF16)

        @pl.loop(1, RING)
        def _(k):
            remote(s_all.at[row], s_all.at[row], r_send.at[0], r_recv.at[0], (wrap(row + k), col, rep)).start()

    def s_end():
        arrived(s_all.at[pl.ds(0, RING - 1)], r_recv.at[0])

    def p_make():
        s_wide = jnp.concatenate([s_all[t] for t in range(RING)], axis=1)
        f_wide = jnp.concatenate(
            [jnp.concatenate([f_all[4 * a + b + 1] for a in range(4)], axis=0) for b in range(3)],
            axis=1,
        )
        p_part = dot(s_wide, xg[...].reshape(RING * 128, 384), ((1,), (0,)))
        p_mine[...] = (p_part + f_wide.astype(F32)).astype(BF16)
        send(p_mine, p_peer, p_send, p_recv, (row, col, 1 - rep))

    def multiply(first, count, base, out):
        ks = slice(256 * first, 256 * (first + count))

        @pl.loop(0, 3)
        def _(n):
            cols = pl.ds(pl.multiple_of(n * 512, 512), 512)
            gs = gg[4 * first:4 * (first + count), :, cols].reshape(256 * count, 512)
            out[:, cols] = (base[:, cols].astype(F32) + dot(xt[:, ks], gs, ((1,), (0,)))).astype(out.dtype)

    def c_one():
        shared(9, OWN)
        shared(1, YM)
        shared(2, YP)
        multiply(OWN, 3, e_in, acc)

    def c_two():
        shared(0, XP)
        shared(3, Y2, FIRST)
        shared(4, Y2, SECOND)
        multiply(Y2, 2, acc, acc)

    def g_rest():
        got(5, YMX)
        got(6, YPX)

    def g_last():
        got(7, Y2X, FIRST)
        got(8, Y2X, SECOND)

    def c_three():
        shared(5, YMX)
        shared(6, YPX)
        multiply(YPX, 2, acc, acc)

    def c_four():
        shared(7, Y2X, FIRST)
        shared(8, Y2X, SECOND)
        multiply(Y2X, 1, acc, comp_ref)

    def t_zero():
        tell(0, right, left)
        tell(3, *plane)

    def t_one():
        told(0, 2)
        tell(1, (row, wrap(col + 4), rep), (row, wrap(col - 4), rep))
        told(3, 4)
        tell(4, *plane)

    def t_three():
        told(1, 2)
        told(4, 4)
        tell(5, *plane)

    def t_four():
        told(5, 4)
        tell(6, here)

    def t_five():
        told(6, 1)

    steps = {f.__name__: f for f in (
        start_x, start_g, t_zero, f_make, t_one, s_near, t_three, f_send_out, s_far, t_four, g_ym,
        g_yp, g_xp, p_xp, f_sum, s_row, g_y2, f_end, s_end, p_make, c_one, g_rest, c_two, t_five, g_last, c_three, c_four,
    )}
    steps.update({"x%d" % k: functools.partial(x_step, k) for k in range(1, 9)})
    for name in ORDER.split():
        steps[name]()
    arrived(p_peer, p_recv)
    p_t = (p_mine[...].astype(F32) + p_peer[...].astype(F32)) * 0.5

    comp_out = pltpu.make_async_copy(comp_ref, comp_hbm, loc_sem.at[0])
    comp_out.start()

    p_high = p_t.astype(BF16)
    p_rest = (p_t - p_high.astype(F32)).astype(BF16)
    p_both = jnp.concatenate([p_high, p_rest], axis=0)
    me = row + RING * rep
    mine = row // 2 + 8 * rep
    owner = core == x

    def piece_at(k):
        chip = lax.rem(k, 8)
        return (2 * chip + lax.rem(chip, 2), col, k // 8)

    for b in range(4):
        cols = slice(384 * b, 384 * b + 384)
        ut = dot(p_both, comp_ref[:, cols], ((1,), (0,)))
        ut = (ut[:RANK] + ut[RANK:]).astype(BF16)
        for a in range(4):
            u_out[4 * a + b] = ut[16 * a:16 * a + 16, :]

    @pl.loop(0, RING)
    def _(k):
        @pl.when(jnp.logical_not(jnp.logical_and(owner, k == mine)))
        def _():
            remote(u_out.at[k], u_in.at[me], u_send.at[0], u_recv.at[0], piece_at(k)).start()

    gram = dot(p_t, p_t, ((1,), (1,)), HIGH)
    gram_mine[...] = jnp.concatenate([gram[:32], gram[32:]], axis=1)

    @pl.loop(1, RING)
    def _(k):
        to = wrap(row + k)
        remote(gram_mine, gram_all.at[row], gr_send, gr_recv, (to, col, rep)).start()

    gram_all[row] = gram_mine[...]

    @pl.when(owner)
    def _():
        u_in[me] = u_out[mine]
        arrived(u_in.at[pl.ds(0, 31)], u_recv.at[0])
        u_own[...] = jnp.sum(u_in[...].astype(F32), axis=0).astype(BF16)

        for dy in (2, 3, 1, 0):
            base = lax.rem(y + dy, 4) * 4

            @pl.loop(0, 8)
            def _(k):
                to = base + lax.rem(k, 4)

                def go():
                    remote(u_own, u_all.at[mine], u_send.at[1], u_recv.at[1], (to, col, k // 4)).start()

                if dy:
                    go()
                else:
                    pl.when(to + RING * (k // 4) != me)(go)

        u_all[mine] = u_own[...]

    arrived(gram_all.at[pl.ds(0, RING - 1)], gr_recv)
    total = jnp.sum(gram_all[...], axis=0)
    gram = jnp.concatenate([total[:, :RANK], total[:, RANK:]], axis=0)
    subl = lax.broadcasted_iota(jnp.int32, (RANK, 128), 0)
    lane = lax.broadcasted_iota(jnp.int32, (RANK, 128), 1)
    mat[...] = jnp.concatenate([gram, (subl == lane)[:, :RANK].astype(F32)], axis=1)

    def pick(rows, k):
        return jnp.sum(jnp.where(lane[:rows.shape[0]] == k, rows, 0.0), axis=1, keepdims=True)

    def eliminate(h, carry):
        k = 2 * h
        m = mat[...]
        row_a, row_b = mat[pl.ds(k, 1), :], mat[pl.ds(k + 1, 1), :]
        col_a, col_b = pick(m, k), pick(m, k + 1)
        corner, cross = pick(row_a, k), pick(row_a, k + 1)
        below, last = pick(row_b, k), pick(row_b, k + 1)
        inverse = 1.0 / corner
        step = below * inverse
        row_b = row_b - step * row_a
        factor_a = col_a * inverse
        factor_b = (col_b - factor_a * cross) / (last - step * cross)
        factor_a = jnp.where(subl[:, :1] > k, factor_a, 0.0)
        factor_b = jnp.where(subl[:, :1] > k + 1, factor_b, 0.0)
        mat[...] = m - factor_a * row_a - factor_b * row_b
        return carry

    lax.fori_loop(0, RANK // 2, eliminate, 0)
    d = jnp.sum(jnp.where(lane == subl, mat[...], 0.0), axis=1, keepdims=True)
    inv_factor = lax.rsqrt(d) * mat[:, RANK:]
    ortho_ref[...] = dot(inv_factor, p_t, ((1,), (0,)), HIGH).astype(BF16)

    @pl.when(owner)
    def _():
        arrived(u_all.at[pl.ds(0, 15)], u_recv.at[1])
        sent(u_out.at[pl.ds(0, 15)], u_send.at[0])
        sent(u_in.at[pl.ds(0, 31)], u_send.at[1])

    @pl.when(jnp.logical_not(owner))
    def _():
        arrived(u_all, u_recv.at[1])
        sent(u_out, u_send.at[0])

    for b in range(4):
        ut = jnp.concatenate([u_all[4 * a + b] for a in range(4)], axis=0).astype(F32) * 0.5
        basis_ref[:, 384 * b:384 * b + 384] = dot(inv_factor, ut, ((1,), (0,)), HIGH)

    comp_out.wait()
    for copy in sends:
        copy.wait_send()
    for k in range(2):
        sent(xg.at[pl.ds(0, 7 * PARTS + PARTS // 2)], x_send.at[k])
    sent(gg.at[pl.ds(0, 14)], g_send)
    sent(gg.at[pl.ds(0, 16)], d_send)
    sent(s_all.at[pl.ds(0, 15)], r_send.at[0])
    sent(gram_all.at[pl.ds(0, 15)], gr_send)


def body(layer_inputs, output_grads, error_prev, basis_prev):
    dma = pltpu.SemaphoreType.DMA
    vmem = pltpu.VMEM
    comp, ortho_t, basis_t = pl.pallas_call(
        kernel,
        out_shape=(
            jax.ShapeDtypeStruct((384, 1536), BF16),
            jax.ShapeDtypeStruct((RANK, 384), BF16),
            jax.ShapeDtypeStruct((RANK, 1536), F32),
        ),
        in_specs=[pl.BlockSpec(memory_space=pl.ANY)] * 4,
        out_specs=[pl.BlockSpec(memory_space=pl.ANY)] + [pl.BlockSpec(memory_space=vmem)] * 2,
        scratch_shapes=[
            vmem((16 * PARTS, ROWS, 384), BF16),
            vmem((32, HALF, 1536), BF16),
            vmem((384, 1536), F32),
            vmem((384, 2048), BF16),
            vmem((384, 1536), BF16),
            vmem((384, 1536), BF16),
            vmem((RANK, 1536), BF16),
            vmem((4, RANK, 128), BF16),
            vmem((4, RANK, 128), BF16),
            vmem((16, 16, 128), BF16),
            vmem((16, 16, 128), BF16),
            vmem((16, 128), BF16),
            vmem((16, 16, 128), BF16),
            vmem((16, RANK, 128), BF16),
            vmem((RANK, 384), BF16),
            vmem((RANK, 384), BF16),
            vmem((32, 128), F32),
            vmem((16, 32, 128), F32),
            vmem((RANK, 128), F32),
            vmem((16, 16, 384), BF16),
            vmem((32, 16, 384), BF16),
            vmem((16, 384), BF16),
            vmem((16, 16, 384), BF16),
            dma((4,)),
            dma((2,)), dma((8 * PARTS,)), dma((8 * PARTS,)),
            dma(()), dma((9,)), dma(()), dma((10,)),
            dma((2, 4)), dma((2, 4)), dma((2,)), dma((2,)), dma((1,)), dma((1,)),
            dma(()), dma(()), dma(()), dma(()), dma((2,)), dma((2,)),
            pltpu.SemaphoreType.REGULAR((7,)),
        ],
        compiler_params=pltpu.CompilerParams(
            collective_id=0, has_side_effects=True, vmem_limit_bytes=60 * 2**20
        ),
        name="powersgd",
    )(layer_inputs.reshape(PARTS, ROWS, 384), output_grads.reshape(2, HALF, 1536), error_prev, basis_prev.T)
    basis_next = basis_t.T
    approx = dot(ortho_t, basis_t.astype(BF16), ((0,), (0,)))
    error_next = (comp.astype(F32) - approx).astype(BF16)
    return (basis_next, error_next[None])


def solution(mesh):
    return jax.shard_map(
        body,
        mesh=mesh,
        in_specs=(
            P("rep", "col", "row"),
            P("rep", "row", "col"),
            P("rep", "row", "col"),
            P("col", None),
        ),
        out_specs=(P("col", None), P("rep", "row", "col")),
        check_vma=False,
    )
```

```python
import functools

import jax
import jax.numpy as jnp
from jax import lax
from jax.experimental import pallas as pl
from jax.experimental.pallas import tpu as pltpu
from jax.sharding import PartitionSpec as P

MESH = pl.DeviceIdType.MESH
HIGH = lax.Precision.HIGHEST
F32 = jnp.float32
BF16 = jnp.bfloat16

RING = 16
HALF = 64
RANK = 64
PARTS = 4
ROWS = 128 // PARTS


ORDER = (
    "s_near start_x start_g t_zero f_make t_one x1 t_three s_far x2 f_send_out t_four x3 "
    "g_ym g_yp g_xp p_xp x4 f_sum s_row x5 g_y2 x6 f_end x7 g_rest s_end x8 p_make "
    "g_last c_one c_two t_five c_three c_four"
)


def dot(a, b, dims, precision=None):
    return lax.dot_general(a, b, (dims, ((), ())), precision=precision, preferred_element_type=F32)


def kernel(
    x_ref, g_ref, e_ref, bt_ref,
    comp_hbm, ortho_ref, basis_ref,
    xg, gg, acc, xt, comp_ref, e_in, bt, s_one, s_two, f_out, f_in, f_own, f_all, s_all, p_mine, p_peer,
    gram_mine, gram_all, mat, u_out, u_in, u_own, u_all,
    loc_sem, x_send, xr_recv, xl_recv, g_send, g_recv, d_send, d_recv,
    s_send, s_recv, f_send, f_recv, r_send, r_recv, p_send, p_recv, gr_send, gr_recv, u_send, u_recv, near,
):
    row, col, rep = lax.axis_index("row"), lax.axis_index("col"), lax.axis_index("rep")
    y, x, core = row // 4, (row // 2) % 2, row % 2

    def at_row(yy, xx, cc):
        return lax.rem(yy + 4, 4) * 4 + xx * 2 + cc

    def wrap(v):
        return lax.rem(v + RING, RING)

    def place_of(dy, dx):
        return dy + dy // 2 - 2 * (dy // 3) + 4 * dx

    def remote(src, dst, ssem, rsem, where):
        return pltpu.make_async_remote_copy(
            src_ref=src, dst_ref=dst, send_sem=ssem, recv_sem=rsem,
            device_id=where, device_id_type=MESH,
        )

    here = (row, col, 1 - rep)
    sends = []

    def send(src, dst, ssem, rsem, where):
        copy = remote(src, dst, ssem, rsem, where)
        copy.start()
        sends.append(copy)

    def arrived(dst, rsem):
        remote(dst, dst, rsem, rsem, here).wait_recv()

    def sent(src, ssem):
        remote(src, src, ssem, ssem, here).wait_send()

    own_g = pltpu.make_async_copy(g_ref, gg.at[pl.ds(0, 2)], loc_sem.at[0])
    own_b = pltpu.make_async_copy(bt_ref, bt, loc_sem.at[1])
    own_x = pltpu.make_async_copy(x_ref, xg.at[pl.ds(PARTS * col, PARTS)], loc_sem.at[2])
    own_e = pltpu.make_async_copy(e_ref.at[0], e_in, loc_sem.at[3])
    for copy in (own_g, own_b, own_x, own_e):
        copy.start()

    barrier = pltpu.get_barrier_semaphore()

    def signal(where):
        pl.semaphore_signal(barrier, inc=1, device_id=where, device_id_type=MESH)

    right, left = (row, wrap(col + 1), rep), (row, wrap(col - 1), rep)
    up, down, side, sib = (
        (at_row(y + 1, x, core), col, rep),
        (at_row(y - 1, x, core), col, rep),
        (at_row(y, 1 - x, core), col, rep),
        (at_row(y, x, 1 - core), col, rep),
    )
    for where in (right, left, up, down, side, sib, here):
        signal(where)
    for k in (2, 3):
        signal((row, wrap(col + k), rep))
        signal((row, wrap(col - k), rep))

    def tell(k, *to):
        for where in to:
            pl.semaphore_signal(near.at[k], inc=1, device_id=where, device_id_type=MESH)

    def told(k, count):
        pl.semaphore_wait(near.at[k], count)

    own_g.wait()
    own_b.wait()
    quarter, group = lax.rem(col, 4), col // 4
    s_one[quarter] = dot(bt[...], gg[0:2].reshape(128, 1536), ((1,), (1,))).astype(BF16)
    own_x.wait()

    pl.semaphore_wait(barrier, 11)
    plane = (up, down, side, sib)

    def x_part(owner, part):
        return xg.at[PARTS * owner + part]

    def x_push(owner, part, k, side):
        ref = x_part(owner, part)
        recv = (xr_recv if side == 0 else xl_recv).at[PARTS * k + part]
        remote(ref, ref, x_send.at[side], recv, right if side == 0 else left).start()

    def x_turn(owner):
        slot = 2 * place_of(lax.rem(owner // 4 - y + 4, 4), lax.rem(owner // 2 + x, 2)) + lax.rem(owner + core, 2)
        xt[:, pl.ds(pl.multiple_of(slot * 128, 128), 128)] = xg[pl.ds(PARTS * owner, PARTS)].reshape(128, 384).T

    def x_step(k):
        frm, to = wrap(col - k), wrap(col + k)
        for i in range(PARTS):
            if k < 8 or i < PARTS // 2:
                arrived(x_part(frm, i), xr_recv.at[PARTS * (k - 1) + i])
                if k < 7 or (k == 7 and i < PARTS // 2):
                    x_push(frm, i, k, 0)
            i = PARTS - 1 - i
            if k < 8 or i >= PARTS // 2:
                arrived(x_part(to, i), xl_recv.at[PARTS * (k - 1) + i])
                if k < 7 or (k == 7 and i >= PARTS // 2):
                    x_push(to, i, k, 1)
        x_turn(frm)
        if k < 8:
            x_turn(to)

    OWN, YP, YM, Y2, XP, YPX, YMX, Y2X = range(8)
    FIRST, SECOND, WHOLE = (0, 1), (1, 1), (0, 2)

    def block(name, part, other=0):
        return gg.at[pl.ds(2 * (2 * name + other) + part[0], part[1])]

    def push(src, k, dst, where, part=WHOLE):
        remote(block(src, part), block(dst, part), g_send, g_recv.at[k], where).start()

    def got(k, name, part=WHOLE):
        arrived(block(name, part), g_recv.at[k])
        share(k, name, part)

    def share(k, name, part=WHOLE):
        remote(block(name, part), block(name, part, 1), d_send, d_recv.at[k], sib).start()

    def shared(k, name, part=WHOLE):
        arrived(block(name, part, 1), d_recv.at[k])

    def start_x():
        for part in range(PARTS):
            x_push(col, part, 0, 0)
            x_push(col, PARTS - 1 - part, 0, 1)
        x_turn(col)

    def start_g():
        push(OWN, 0, XP, side)
        push(OWN, 1, YM, up)
        push(OWN, 2, YP, down)
        share(9, OWN)

    def g_ym():
        got(1, YM)
        push(YM, 3, Y2, up, FIRST)

    def g_yp():
        got(2, YP)
        push(YP, 4, Y2, down, SECOND)

    def g_xp():
        got(0, XP)

    def p_xp():
        push(XP, 5, YMX, up)
        push(XP, 6, YPX, down)

    def g_y2():
        got(3, Y2, FIRST)
        push(Y2, 7, Y2X, side, FIRST)
        got(4, Y2, SECOND)
        push(Y2, 8, Y2X, side, SECOND)

    f_owner = quarter > 0
    f_count = 12

    def f_make():
        own_e.wait()
        ft = dot(bt[...], e_in[...], ((1,), (1,))).astype(BF16)
        for a in range(4):
            for b in range(3):
                f_out[4 * a + b + 1] = ft[16 * a:16 * a + 16, 128 * b:128 * b + 128]

    def f_send_out():
        @pl.loop(1, RING)
        def _(k):
            to = wrap(col + k)

            @pl.when(lax.rem(to, 4) > 0)
            def _():
                remote(f_out.at[to], f_in.at[col], f_send.at[0], f_recv.at[0], (row, to, rep)).start()

    def f_sum():
        @pl.when(f_owner)
        def _():
            f_in[col] = f_out[col]
            arrived(f_in.at[pl.ds(0, RING - 1)], f_recv.at[0])
            f_own[...] = jnp.sum(f_in[...].astype(F32), axis=0).astype(BF16)

            @pl.loop(1, RING)
            def _(k):
                remote(f_own, f_all.at[col], f_send.at[1], f_recv.at[1], (row, wrap(col + k), rep)).start()

            f_all[col] = f_own[...]
            sent(f_out.at[pl.ds(0, f_count - 1)], f_send.at[0])

    def f_end():
        @pl.when(f_owner)
        def _():
            arrived(f_all.at[pl.ds(0, f_count - 1)], f_recv.at[1])
            sent(f_in.at[pl.ds(0, RING - 1)], f_send.at[1])

        @pl.when(jnp.logical_not(f_owner))
        def _():
            arrived(f_all.at[pl.ds(0, f_count)], f_recv.at[1])
            sent(f_out.at[pl.ds(0, f_count)], f_send.at[0])

    def s_near():
        for k in range(1, 4):
            to = lax.rem(quarter + k, 4)
            send(s_one.at[quarter], s_one.at[quarter], s_send.at[0, k], s_recv.at[0, k], (row, group * 4 + to, rep))

    def s_far():
        for k in range(1, 4):
            arrived(s_one.at[lax.rem(quarter + 4 - k, 4)], s_recv.at[0, k])
        s_two[group] = jnp.sum(s_one[...].astype(F32), axis=0).astype(BF16)
        for k in range(1, 4):
            to = lax.rem(group + k, 4)
            send(s_two.at[group], s_two.at[group], s_send.at[1, k], s_recv.at[1, k], (row, to * 4 + quarter, rep))

    def s_row():
        for k in range(1, 4):
            arrived(s_two.at[lax.rem(group + 4 - k, 4)], s_recv.at[1, k])
        s_all[row] = jnp.sum(s_two[...].astype(F32), axis=0).astype(BF16)

        @pl.loop(1, RING)
        def _(k):
            remote(s_all.at[row], s_all.at[row], r_send.at[0], r_recv.at[0], (wrap(row + k), col, rep)).start()

    def s_end():
        arrived(s_all.at[pl.ds(0, RING - 1)], r_recv.at[0])

    def p_make():
        s_wide = jnp.concatenate([s_all[t] for t in range(RING)], axis=1)
        f_wide = jnp.concatenate(
            [jnp.concatenate([f_all[4 * a + b + 1] for a in range(4)], axis=0) for b in range(3)],
            axis=1,
        )
        p_part = dot(s_wide, xg[...].reshape(RING * 128, 384), ((1,), (0,)))
        p_mine[...] = (p_part + f_wide.astype(F32)).astype(BF16)
        send(p_mine, p_peer, p_send, p_recv, (row, col, 1 - rep))

    def multiply(first, count, base, out):
        ks = slice(256 * first, 256 * (first + count))

        @pl.loop(0, 3)
        def _(n):
            cols = pl.ds(pl.multiple_of(n * 512, 512), 512)
            gs = gg[4 * first:4 * (first + count), :, cols].reshape(256 * count, 512)
            out[:, cols] = (base[:, cols].astype(F32) + dot(xt[:, ks], gs, ((1,), (0,)))).astype(out.dtype)

    def c_one():
        shared(9, OWN)
        shared(1, YM)
        shared(2, YP)
        multiply(OWN, 3, e_in, acc)

    def c_two():
        shared(0, XP)
        shared(3, Y2, FIRST)
        shared(4, Y2, SECOND)
        multiply(Y2, 2, acc, acc)

    def g_rest():
        got(5, YMX)
        got(6, YPX)

    def g_last():
        got(7, Y2X, FIRST)
        got(8, Y2X, SECOND)

    def c_three():
        shared(5, YMX)
        shared(6, YPX)
        multiply(YPX, 2, acc, acc)

    def c_four():
        shared(7, Y2X, FIRST)
        shared(8, Y2X, SECOND)
        multiply(Y2X, 1, acc, comp_ref)

    def t_zero():
        tell(0, right, left)
        tell(3, *plane)

    def t_one():
        told(0, 2)
        tell(1, (row, wrap(col + 4), rep), (row, wrap(col - 4), rep))
        told(3, 4)
        tell(4, *plane)

    def t_three():
        told(1, 2)
        told(4, 4)
        tell(5, *plane)

    def t_four():
        told(5, 4)
        tell(6, here)

    def t_five():
        told(6, 1)

    steps = {f.__name__: f for f in (
        start_x, start_g, t_zero, f_make, t_one, s_near, t_three, f_send_out, s_far, t_four, g_ym,
        g_yp, g_xp, p_xp, f_sum, s_row, g_y2, f_end, s_end, p_make, c_one, g_rest, c_two, t_five, g_last, c_three, c_four,
    )}
    steps.update({"x%d" % k: functools.partial(x_step, k) for k in range(1, 9)})
    for name in ORDER.split():
        steps[name]()
    arrived(p_peer, p_recv)
    p_t = (p_mine[...].astype(F32) + p_peer[...].astype(F32)) * 0.5

    comp_out = pltpu.make_async_copy(comp_ref, comp_hbm, loc_sem.at[0])
    comp_out.start()

    p_high = p_t.astype(BF16)
    p_rest = (p_t - p_high.astype(F32)).astype(BF16)
    p_both = jnp.concatenate([p_high, p_rest], axis=0)
    me = row + RING * rep
    mine = row // 2 + 8 * rep
    owner = core == x

    def piece_at(k):
        chip = lax.rem(k, 8)
        return (2 * chip + lax.rem(chip, 2), col, k // 8)

    for b in range(4):
        cols = slice(384 * b, 384 * b + 384)
        ut = dot(p_both, comp_ref[:, cols], ((1,), (0,)))
        ut = (ut[:RANK] + ut[RANK:]).astype(BF16)
        for a in range(4):
            u_out[4 * a + b] = ut[16 * a:16 * a + 16, :]

    @pl.loop(0, RING)
    def _(k):
        @pl.when(jnp.logical_not(jnp.logical_and(owner, k == mine)))
        def _():
            remote(u_out.at[k], u_in.at[me], u_send.at[0], u_recv.at[0], piece_at(k)).start()

    gram = dot(p_t, p_t, ((1,), (1,)), HIGH)
    gram_mine[...] = jnp.concatenate([gram[:32], gram[32:]], axis=1)

    @pl.loop(1, RING)
    def _(k):
        to = wrap(row + k)
        remote(gram_mine, gram_all.at[row], gr_send, gr_recv, (to, col, rep)).start()

    gram_all[row] = gram_mine[...]

    @pl.when(owner)
    def _():
        u_in[me] = u_out[mine]
        arrived(u_in.at[pl.ds(0, 31)], u_recv.at[0])
        u_own[...] = jnp.sum(u_in[...].astype(F32), axis=0).astype(BF16)

        for dy in (2, 3, 1, 0):
            base = lax.rem(y + dy, 4) * 4

            @pl.loop(0, 8)
            def _(k):
                to = base + lax.rem(k, 4)

                def go():
                    remote(u_own, u_all.at[mine], u_send.at[1], u_recv.at[1], (to, col, k // 4)).start()

                if dy:
                    go()
                else:
                    pl.when(to + RING * (k // 4) != me)(go)

        u_all[mine] = u_own[...]

    arrived(gram_all.at[pl.ds(0, RING - 1)], gr_recv)
    total = jnp.sum(gram_all[...], axis=0)
    gram = jnp.concatenate([total[:, :RANK], total[:, RANK:]], axis=0)
    subl = lax.broadcasted_iota(jnp.int32, (RANK, 128), 0)
    lane = lax.broadcasted_iota(jnp.int32, (RANK, 128), 1)
    mat[...] = jnp.concatenate([gram, (subl == lane)[:, :RANK].astype(F32)], axis=1)

    def pick(rows, k):
        return jnp.sum(jnp.where(lane[:rows.shape[0]] == k, rows, 0.0), axis=1, keepdims=True)

    def eliminate(h, carry):
        k = 2 * h
        m = mat[...]
        row_a, row_b = mat[pl.ds(k, 1), :], mat[pl.ds(k + 1, 1), :]
        col_a, col_b = pick(m, k), pick(m, k + 1)
        corner, cross = pick(row_a, k), pick(row_a, k + 1)
        below, last = pick(row_b, k), pick(row_b, k + 1)
        inverse = 1.0 / corner
        step = below * inverse
        row_b = row_b - step * row_a
        factor_a = col_a * inverse
        factor_b = (col_b - factor_a * cross) / (last - step * cross)
        factor_a = jnp.where(subl[:, :1] > k, factor_a, 0.0)
        factor_b = jnp.where(subl[:, :1] > k + 1, factor_b, 0.0)
        mat[...] = m - factor_a * row_a - factor_b * row_b
        return carry

    lax.fori_loop(0, RANK // 2, eliminate, 0)
    d = jnp.sum(jnp.where(lane == subl, mat[...], 0.0), axis=1, keepdims=True)
    inv_factor = lax.rsqrt(d) * mat[:, RANK:]
    ortho_ref[...] = dot(inv_factor, p_t, ((1,), (0,)), HIGH).astype(BF16)

    @pl.when(owner)
    def _():
        arrived(u_all.at[pl.ds(0, 15)], u_recv.at[1])
        sent(u_out.at[pl.ds(0, 15)], u_send.at[0])
        sent(u_in.at[pl.ds(0, 31)], u_send.at[1])

    @pl.when(jnp.logical_not(owner))
    def _():
        arrived(u_all, u_recv.at[1])
        sent(u_out, u_send.at[0])

    for b in range(4):
        ut = jnp.concatenate([u_all[4 * a + b] for a in range(4)], axis=0).astype(F32) * 0.5
        basis_ref[:, 384 * b:384 * b + 384] = dot(inv_factor, ut, ((1,), (0,)), HIGH)

    comp_out.wait()
    for copy in sends:
        copy.wait_send()
    for k in range(2):
        sent(xg.at[pl.ds(0, 7 * PARTS + PARTS // 2)], x_send.at[k])
    sent(gg.at[pl.ds(0, 14)], g_send)
    sent(gg.at[pl.ds(0, 16)], d_send)
    sent(s_all.at[pl.ds(0, 15)], r_send.at[0])
    sent(gram_all.at[pl.ds(0, 15)], gr_send)


def body(layer_inputs, output_grads, error_prev, basis_prev):
    dma = pltpu.SemaphoreType.DMA
    vmem = pltpu.VMEM
    comp, ortho_t, basis_t = pl.pallas_call(
        kernel,
        out_shape=(
            jax.ShapeDtypeStruct((384, 1536), BF16),
            jax.ShapeDtypeStruct((RANK, 384), BF16),
            jax.ShapeDtypeStruct((RANK, 1536), F32),
        ),
        in_specs=[pl.BlockSpec(memory_space=pl.ANY)] * 4,
        out_specs=[pl.BlockSpec(memory_space=pl.ANY)] + [pl.BlockSpec(memory_space=vmem)] * 2,
        scratch_shapes=[
            vmem((16 * PARTS, ROWS, 384), BF16),
            vmem((32, HALF, 1536), BF16),
            vmem((384, 1536), F32),
            vmem((384, 2048), BF16),
            vmem((384, 1536), BF16),
            vmem((384, 1536), BF16),
            vmem((RANK, 1536), BF16),
            vmem((4, RANK, 128), BF16),
            vmem((4, RANK, 128), BF16),
            vmem((16, 16, 128), BF16),
            vmem((16, 16, 128), BF16),
            vmem((16, 128), BF16),
            vmem((16, 16, 128), BF16),
            vmem((16, RANK, 128), BF16),
            vmem((RANK, 384), BF16),
            vmem((RANK, 384), BF16),
            vmem((32, 128), F32),
            vmem((16, 32, 128), F32),
            vmem((RANK, 128), F32),
            vmem((16, 16, 384), BF16),
            vmem((32, 16, 384), BF16),
            vmem((16, 384), BF16),
            vmem((16, 16, 384), BF16),
            dma((4,)),
            dma((2,)), dma((8 * PARTS,)), dma((8 * PARTS,)),
            dma(()), dma((9,)), dma(()), dma((10,)),
            dma((2, 4)), dma((2, 4)), dma((2,)), dma((2,)), dma((1,)), dma((1,)),
            dma(()), dma(()), dma(()), dma(()), dma((2,)), dma((2,)),
            pltpu.SemaphoreType.REGULAR((7,)),
        ],
        compiler_params=pltpu.CompilerParams(
            collective_id=0, has_side_effects=True, vmem_limit_bytes=60 * 2**20
        ),
        name="powersgd",
    )(layer_inputs.reshape(PARTS, ROWS, 384), output_grads.reshape(2, HALF, 1536), error_prev, basis_prev.T)
    basis_next = basis_t.T
    approx = dot(ortho_t, basis_t.astype(BF16), ((0,), (0,)))
    error_next = (comp.astype(F32) - approx).astype(BF16)
    return (basis_next, error_next[None])


def solution(mesh):
    return jax.shard_map(
        body,
        mesh=mesh,
        in_specs=(
            P("rep", "col", "row"),
            P("rep", "row", "col"),
            P("rep", "row", "col"),
            P("col", None),
        ),
        out_specs=(P("col", None), P("rep", "row", "col")),
        check_vma=False,
    )
```

```python
import jax
import jax.numpy as jnp
from jax import lax
from jax.experimental import pallas as pl
from jax.experimental.pallas import tpu as pltpu
from jax.sharding import PartitionSpec as P

MESH = pl.DeviceIdType.MESH
HIGH = lax.Precision.HIGHEST
F32 = jnp.float32
BF16 = jnp.bfloat16

RING = 16
HALF = 64
RANK = 64
PARTS = 4
ROWS = 128 // PARTS


def dot(a, b, dims, precision=None):
    return lax.dot_general(a, b, (dims, ((), ())), precision=precision, preferred_element_type=F32)


def kernel(
    x_ref, g_ref, e_ref, bt_ref,
    comp_hbm, ortho_ref, basis_ref,
    xg, gg, acc, xt, comp_ref, e_in, bt, s_one, s_two, f_out, f_in, f_own, f_all, s_all, p_mine, p_peer,
    gram_mine, gram_all, mat, u_out, u_in, u_own, u_all,
    loc_sem, x_send, xr_recv, xl_recv, g_send, g_recv, d_send, d_recv,
    s_send, s_recv, f_send, f_recv, r_send, r_recv, p_send, p_recv, gr_send, gr_recv, u_send, u_recv, near,
):
    row, col, rep = lax.axis_index("row"), lax.axis_index("col"), lax.axis_index("rep")
    y, x, core = row // 4, (row // 2) % 2, row % 2

    def at_row(yy, xx, cc):
        return lax.rem(yy + 4, 4) * 4 + xx * 2 + cc

    def wrap(v):
        return lax.rem(v + RING, RING)

    def place_of(dy, dx):
        return dy + dy // 2 - 2 * (dy // 3) + 4 * dx

    def remote(src, dst, ssem, rsem, where):
        return pltpu.make_async_remote_copy(
            src_ref=src, dst_ref=dst, send_sem=ssem, recv_sem=rsem,
            device_id=where, device_id_type=MESH,
        )

    here = (row, col, 1 - rep)
    sends = []

    def send(src, dst, ssem, rsem, where):
        copy = remote(src, dst, ssem, rsem, where)
        copy.start()
        sends.append(copy)

    def arrived(dst, rsem):
        remote(dst, dst, rsem, rsem, here).wait_recv()

    def sent(src, ssem):
        remote(src, src, ssem, ssem, here).wait_send()

    own_g = pltpu.make_async_copy(g_ref, gg.at[pl.ds(0, 2)], loc_sem.at[0])
    own_b = pltpu.make_async_copy(bt_ref, bt, loc_sem.at[1])
    own_x = pltpu.make_async_copy(x_ref, xg.at[pl.ds(PARTS * col, PARTS)], loc_sem.at[2])
    own_e = pltpu.make_async_copy(e_ref.at[0], e_in, loc_sem.at[3])
    for copy in (own_g, own_b, own_x, own_e):
        copy.start()

    barrier = pltpu.get_barrier_semaphore()

    def signal(where):
        pl.semaphore_signal(barrier, inc=1, device_id=where, device_id_type=MESH)

    right, left = (row, wrap(col + 1), rep), (row, wrap(col - 1), rep)
    up, down, side, sib = (
        (at_row(y + 1, x, core), col, rep),
        (at_row(y - 1, x, core), col, rep),
        (at_row(y, 1 - x, core), col, rep),
        (at_row(y, x, 1 - core), col, rep),
    )
    for where in (right, left, up, down, side, sib, here):
        signal(where)
    for k in (2, 3):
        signal((row, wrap(col + k), rep))
        signal((row, wrap(col - k), rep))

    def tell(k, *to):
        for where in to:
            pl.semaphore_signal(near.at[k], inc=1, device_id=where, device_id_type=MESH)

    def told(k, count):
        pl.semaphore_wait(near.at[k], count)

    own_g.wait()
    own_b.wait()
    quarter, group = lax.rem(col, 4), col // 4
    s_one[quarter] = dot(bt[...], gg[0:2].reshape(128, 1536), ((1,), (1,))).astype(BF16)
    own_x.wait()

    pl.semaphore_wait(barrier, 11)
    plane = (up, down, side, sib)

    def x_part(owner, part):
        return xg.at[PARTS * owner + part]

    def x_push(owner, part, k, side):
        ref = x_part(owner, part)
        recv = (xr_recv if side == 0 else xl_recv).at[PARTS * k + part]
        remote(ref, ref, x_send.at[side], recv, right if side == 0 else left).start()

    def x_turn(owner):
        slot = 2 * place_of(lax.rem(owner // 4 - y + 4, 4), lax.rem(owner // 2 + x, 2)) + lax.rem(owner + core, 2)
        xt[:, pl.ds(pl.multiple_of(slot * 128, 128), 128)] = xg[pl.ds(PARTS * owner, PARTS)].reshape(128, 384).T

    def x_step(k):
        frm, to = wrap(col - k), wrap(col + k)
        for i in range(PARTS):
            if k < 8 or i < PARTS // 2:
                arrived(x_part(frm, i), xr_recv.at[PARTS * (k - 1) + i])
                if k < 7 or (k == 7 and i < PARTS // 2):
                    x_push(frm, i, k, 0)
            i = PARTS - 1 - i
            if k < 8 or i >= PARTS // 2:
                arrived(x_part(to, i), xl_recv.at[PARTS * (k - 1) + i])
                if k < 7 or (k == 7 and i >= PARTS // 2):
                    x_push(to, i, k, 1)
        x_turn(frm)
        if k < 8:
            x_turn(to)

    OWN, YP, YM, Y2, XP, YPX, YMX, Y2X = range(8)
    FIRST, SECOND, WHOLE = (0, 1), (1, 1), (0, 2)

    def block(name, part, other=0):
        return gg.at[pl.ds(2 * (2 * name + other) + part[0], part[1])]

    def push(src, k, dst, where, part=WHOLE):
        remote(block(src, part), block(dst, part), g_send, g_recv.at[k], where).start()

    def got(k, name, part=WHOLE):
        arrived(block(name, part), g_recv.at[k])
        share(k, name, part)

    def share(k, name, part=WHOLE):
        remote(block(name, part), block(name, part, 1), d_send, d_recv.at[k], sib).start()

    def shared(k, name, part=WHOLE):
        arrived(block(name, part, 1), d_recv.at[k])

    def start_x():
        for part in range(PARTS):
            x_push(col, part, 0, 0)
            x_push(col, PARTS - 1 - part, 0, 1)
        x_turn(col)

    def start_g():
        push(OWN, 0, XP, side)
        push(OWN, 1, YM, up)
        push(OWN, 2, YP, down)
        share(9, OWN)

    def g_ym():
        got(1, YM)
        push(YM, 3, Y2, up, FIRST)

    def g_yp():
        got(2, YP)
        push(YP, 4, Y2, down, SECOND)

    def g_xp():
        got(0, XP)

    def p_xp():
        push(XP, 5, YMX, up)
        push(XP, 6, YPX, down)

    def g_y2():
        got(3, Y2, FIRST)
        push(Y2, 7, Y2X, side, FIRST)
        got(4, Y2, SECOND)
        push(Y2, 8, Y2X, side, SECOND)

    f_owner = quarter > 0
    f_count = 12

    def f_make():
        own_e.wait()
        ft = dot(bt[...], e_in[...], ((1,), (1,))).astype(BF16)
        for a in range(4):
            for b in range(3):
                f_out[4 * a + b + 1] = ft[16 * a:16 * a + 16, 128 * b:128 * b + 128]

    def f_send_out():
        @pl.loop(1, RING)
        def _(k):
            to = wrap(col + k)

            @pl.when(lax.rem(to, 4) > 0)
            def _():
                remote(f_out.at[to], f_in.at[col], f_send.at[0], f_recv.at[0], (row, to, rep)).start()

    def f_sum():
        @pl.when(f_owner)
        def _():
            f_in[col] = f_out[col]
            arrived(f_in.at[pl.ds(0, RING - 1)], f_recv.at[0])
            f_own[...] = jnp.sum(f_in[...].astype(F32), axis=0).astype(BF16)

            @pl.loop(1, RING)
            def _(k):
                remote(f_own, f_all.at[col], f_send.at[1], f_recv.at[1], (row, wrap(col + k), rep)).start()

            f_all[col] = f_own[...]
            sent(f_out.at[pl.ds(0, f_count - 1)], f_send.at[0])

    def f_end():
        @pl.when(f_owner)
        def _():
            arrived(f_all.at[pl.ds(0, f_count - 1)], f_recv.at[1])
            sent(f_in.at[pl.ds(0, RING - 1)], f_send.at[1])

        @pl.when(jnp.logical_not(f_owner))
        def _():
            arrived(f_all.at[pl.ds(0, f_count)], f_recv.at[1])
            sent(f_out.at[pl.ds(0, f_count)], f_send.at[0])

    def s_near():
        for k in range(1, 4):
            to = lax.rem(quarter + k, 4)
            send(s_one.at[quarter], s_one.at[quarter], s_send.at[0, k], s_recv.at[0, k], (row, group * 4 + to, rep))

    def s_far():
        for k in range(1, 4):
            arrived(s_one.at[lax.rem(quarter + 4 - k, 4)], s_recv.at[0, k])
        s_two[group] = jnp.sum(s_one[...].astype(F32), axis=0).astype(BF16)
        for k in range(1, 4):
            to = lax.rem(group + k, 4)
            send(s_two.at[group], s_two.at[group], s_send.at[1, k], s_recv.at[1, k], (row, to * 4 + quarter, rep))

    def s_row():
        for k in range(1, 4):
            arrived(s_two.at[lax.rem(group + 4 - k, 4)], s_recv.at[1, k])
        s_all[row] = jnp.sum(s_two[...].astype(F32), axis=0).astype(BF16)

        @pl.loop(1, RING)
        def _(k):
            remote(s_all.at[row], s_all.at[row], r_send.at[0], r_recv.at[0], (wrap(row + k), col, rep)).start()

    def s_end():
        arrived(s_all.at[pl.ds(0, RING - 1)], r_recv.at[0])

    def p_make():
        s_wide = jnp.concatenate([s_all[t] for t in range(RING)], axis=1)
        f_wide = jnp.concatenate(
            [jnp.concatenate([f_all[4 * a + b + 1] for a in range(4)], axis=0) for b in range(3)],
            axis=1,
        )
        p_part = dot(s_wide, xg[...].reshape(RING * 128, 384), ((1,), (0,)))
        p_mine[...] = (p_part + f_wide.astype(F32)).astype(BF16)
        send(p_mine, p_peer, p_send, p_recv, (row, col, 1 - rep))

    def multiply(first, count, base, out):
        ks = slice(256 * first, 256 * (first + count))

        @pl.loop(0, 3)
        def _(n):
            cols = pl.ds(pl.multiple_of(n * 512, 512), 512)
            gs = gg[4 * first:4 * (first + count), :, cols].reshape(256 * count, 512)
            out[:, cols] = (base[:, cols].astype(F32) + dot(xt[:, ks], gs, ((1,), (0,)))).astype(out.dtype)

    def c_one():
        shared(9, OWN)
        shared(1, YM)
        shared(2, YP)
        multiply(OWN, 3, e_in, acc)

    def c_two():
        shared(0, XP)
        shared(3, Y2, FIRST)
        shared(4, Y2, SECOND)
        multiply(Y2, 2, acc, acc)

    def g_rest():
        got(5, YMX)
        got(6, YPX)

    def g_last():
        got(7, Y2X, FIRST)
        got(8, Y2X, SECOND)

    def c_three():
        shared(5, YMX)
        shared(6, YPX)
        multiply(YPX, 2, acc, acc)

    def c_four():
        shared(7, Y2X, FIRST)
        shared(8, Y2X, SECOND)
        multiply(Y2X, 1, acc, comp_ref)

    def t_zero():
        tell(0, right, left)
        tell(3, *plane)

    def t_one():
        told(0, 2)
        tell(1, (row, wrap(col + 4), rep), (row, wrap(col - 4), rep))
        told(3, 4)
        tell(4, *plane)

    def t_three():
        told(1, 2)
        told(4, 4)
        tell(5, *plane)

    def t_four():
        told(5, 4)
        tell(6, here)

    def t_five():
        told(6, 1)

    s_near()
    start_x()
    start_g()
    t_zero()
    f_make()
    t_one()
    x_step(1)
    t_three()
    s_far()
    x_step(2)
    f_send_out()
    t_four()
    x_step(3)
    g_ym()
    g_yp()
    g_xp()
    p_xp()
    x_step(4)
    f_sum()
    s_row()
    x_step(5)
    g_y2()
    x_step(6)
    f_end()
    x_step(7)
    g_rest()
    s_end()
    x_step(8)
    p_make()
    g_last()
    c_one()
    c_two()
    t_five()
    c_three()
    c_four()
    arrived(p_peer, p_recv)
    p_t = (p_mine[...].astype(F32) + p_peer[...].astype(F32)) * 0.5

    comp_out = pltpu.make_async_copy(comp_ref, comp_hbm, loc_sem.at[0])
    comp_out.start()

    p_high = p_t.astype(BF16)
    p_rest = (p_t - p_high.astype(F32)).astype(BF16)
    p_both = jnp.concatenate([p_high, p_rest], axis=0)
    me = row + RING * rep
    mine = row // 2 + 8 * rep
    owner = core == x

    def piece_at(k):
        chip = lax.rem(k, 8)
        return (2 * chip + lax.rem(chip, 2), col, k // 8)

    for b in range(4):
        cols = slice(384 * b, 384 * b + 384)
        ut = dot(p_both, comp_ref[:, cols], ((1,), (0,)))
        ut = (ut[:RANK] + ut[RANK:]).astype(BF16)
        for a in range(4):
            u_out[4 * a + b] = ut[16 * a:16 * a + 16, :]

    @pl.loop(0, RING)
    def _(k):
        @pl.when(jnp.logical_not(jnp.logical_and(owner, k == mine)))
        def _():
            remote(u_out.at[k], u_in.at[me], u_send.at[0], u_recv.at[0], piece_at(k)).start()

    gram = dot(p_t, p_t, ((1,), (1,)), HIGH)
    gram_mine[...] = jnp.concatenate([gram[:32], gram[32:]], axis=1)

    @pl.loop(1, RING)
    def _(k):
        to = wrap(row + k)
        remote(gram_mine, gram_all.at[row], gr_send, gr_recv, (to, col, rep)).start()

    gram_all[row] = gram_mine[...]

    @pl.when(owner)
    def _():
        u_in[me] = u_out[mine]
        arrived(u_in.at[pl.ds(0, 31)], u_recv.at[0])
        u_own[...] = jnp.sum(u_in[...].astype(F32), axis=0).astype(BF16)

        for dy in (2, 3, 1, 0):
            base = lax.rem(y + dy, 4) * 4

            @pl.loop(0, 8)
            def _(k):
                to = base + lax.rem(k, 4)

                def go():
                    remote(u_own, u_all.at[mine], u_send.at[1], u_recv.at[1], (to, col, k // 4)).start()

                if dy:
                    go()
                else:
                    pl.when(to + RING * (k // 4) != me)(go)

        u_all[mine] = u_own[...]

    arrived(gram_all.at[pl.ds(0, RING - 1)], gr_recv)
    total = jnp.sum(gram_all[...], axis=0)
    gram = jnp.concatenate([total[:, :RANK], total[:, RANK:]], axis=0)
    subl = lax.broadcasted_iota(jnp.int32, (RANK, 128), 0)
    lane = lax.broadcasted_iota(jnp.int32, (RANK, 128), 1)
    mat[...] = jnp.concatenate([gram, (subl == lane)[:, :RANK].astype(F32)], axis=1)

    def pick(rows, k):
        return jnp.sum(jnp.where(lane[:rows.shape[0]] == k, rows, 0.0), axis=1, keepdims=True)

    def eliminate(h, carry):
        k = 2 * h
        m = mat[...]
        row_a, row_b = mat[pl.ds(k, 1), :], mat[pl.ds(k + 1, 1), :]
        col_a, col_b = pick(m, k), pick(m, k + 1)
        corner, cross = pick(row_a, k), pick(row_a, k + 1)
        below, last = pick(row_b, k), pick(row_b, k + 1)
        inverse = 1.0 / corner
        step = below * inverse
        row_b = row_b - step * row_a
        factor_a = col_a * inverse
        factor_b = (col_b - factor_a * cross) / (last - step * cross)
        factor_a = jnp.where(subl[:, :1] > k, factor_a, 0.0)
        factor_b = jnp.where(subl[:, :1] > k + 1, factor_b, 0.0)
        mat[...] = m - factor_a * row_a - factor_b * row_b
        return carry

    lax.fori_loop(0, RANK // 2, eliminate, 0)
    d = jnp.sum(jnp.where(lane == subl, mat[...], 0.0), axis=1, keepdims=True)
    inv_factor = lax.rsqrt(d) * mat[:, RANK:]
    ortho_ref[...] = dot(inv_factor, p_t, ((1,), (0,)), HIGH).astype(BF16)

    @pl.when(owner)
    def _():
        arrived(u_all.at[pl.ds(0, 15)], u_recv.at[1])
        sent(u_out.at[pl.ds(0, 15)], u_send.at[0])
        sent(u_in.at[pl.ds(0, 31)], u_send.at[1])

    @pl.when(jnp.logical_not(owner))
    def _():
        arrived(u_all, u_recv.at[1])
        sent(u_out, u_send.at[0])

    for b in range(4):
        ut = jnp.concatenate([u_all[4 * a + b] for a in range(4)], axis=0).astype(F32) * 0.5
        basis_ref[:, 384 * b:384 * b + 384] = dot(inv_factor, ut, ((1,), (0,)), HIGH)

    comp_out.wait()
    for copy in sends:
        copy.wait_send()
    for k in range(2):
        sent(xg.at[pl.ds(0, 7 * PARTS + PARTS // 2)], x_send.at[k])
    sent(gg.at[pl.ds(0, 14)], g_send)
    sent(gg.at[pl.ds(0, 16)], d_send)
    sent(s_all.at[pl.ds(0, 15)], r_send.at[0])
    sent(gram_all.at[pl.ds(0, 15)], gr_send)


def body(layer_inputs, output_grads, error_prev, basis_prev):
    dma = pltpu.SemaphoreType.DMA
    vmem = pltpu.VMEM
    comp, ortho_t, basis_t = pl.pallas_call(
        kernel,
        out_shape=(
            jax.ShapeDtypeStruct((384, 1536), BF16),
            jax.ShapeDtypeStruct((RANK, 384), BF16),
            jax.ShapeDtypeStruct((RANK, 1536), F32),
        ),
        in_specs=[pl.BlockSpec(memory_space=pl.ANY)] * 4,
        out_specs=[pl.BlockSpec(memory_space=pl.ANY)] + [pl.BlockSpec(memory_space=vmem)] * 2,
        scratch_shapes=[
            vmem((16 * PARTS, ROWS, 384), BF16),
            vmem((32, HALF, 1536), BF16),
            vmem((384, 1536), F32),
            vmem((384, 2048), BF16),
            vmem((384, 1536), BF16),
            vmem((384, 1536), BF16),
            vmem((RANK, 1536), BF16),
            vmem((4, RANK, 128), BF16),
            vmem((4, RANK, 128), BF16),
            vmem((16, 16, 128), BF16),
            vmem((16, 16, 128), BF16),
            vmem((16, 128), BF16),
            vmem((16, 16, 128), BF16),
            vmem((16, RANK, 128), BF16),
            vmem((RANK, 384), BF16),
            vmem((RANK, 384), BF16),
            vmem((32, 128), F32),
            vmem((16, 32, 128), F32),
            vmem((RANK, 128), F32),
            vmem((16, 16, 384), BF16),
            vmem((32, 16, 384), BF16),
            vmem((16, 384), BF16),
            vmem((16, 16, 384), BF16),
            dma((4,)),
            dma((2,)), dma((8 * PARTS,)), dma((8 * PARTS,)),
            dma(()), dma((9,)), dma(()), dma((10,)),
            dma((2, 4)), dma((2, 4)), dma((2,)), dma((2,)), dma((1,)), dma((1,)),
            dma(()), dma(()), dma(()), dma(()), dma((2,)), dma((2,)),
            pltpu.SemaphoreType.REGULAR((7,)),
        ],
        compiler_params=pltpu.CompilerParams(
            collective_id=0, has_side_effects=True, vmem_limit_bytes=60 * 2**20
        ),
        name="powersgd",
    )(layer_inputs.reshape(PARTS, ROWS, 384), output_grads.reshape(2, HALF, 1536), error_prev, basis_prev.T)
    basis_next = basis_t.T
    approx = dot(ortho_t, basis_t.astype(BF16), ((0,), (0,)))
    error_next = (comp.astype(F32) - approx).astype(BF16)
    return (basis_next, error_next[None])


def solution(mesh):
    return jax.shard_map(
        body,
        mesh=mesh,
        in_specs=(
            P("rep", "col", "row"),
            P("rep", "row", "col"),
            P("rep", "row", "col"),
            P("col", None),
        ),
        out_specs=(P("col", None), P("rep", "row", "col")),
        check_vma=False,
    )
```

```python
import jax
import jax.numpy as jnp
from jax import lax
from jax.experimental import pallas as pl
from jax.experimental.pallas import tpu as pltpu
from jax.sharding import PartitionSpec as P

MESH = pl.DeviceIdType.MESH
HIGH = lax.Precision.HIGHEST
F32 = jnp.float32
BF16 = jnp.bfloat16

RING = 16
HALF = 64
RANK = 64
PARTS = 4
ROWS = 128 // PARTS


def dot(a, b, dims, precision=None):
    return lax.dot_general(a, b, (dims, ((), ())), precision=precision, preferred_element_type=F32)


def kernel(
    x_ref, g_ref, e_ref, bt_ref,
    comp_hbm, ortho_ref, basis_ref,
    xg, gg, acc, xt, comp_ref, e_in, bt, s_one, s_two, f_out, f_in, f_own, f_all, s_all, p_mine, p_peer,
    gram_mine, gram_all, mat, u_out, u_in, u_own, u_all,
    loc_sem, x_send, xr_recv, xl_recv, g_send, g_recv, d_send, d_recv,
    s_send, s_recv, f_send, f_recv, r_send, r_recv, p_send, p_recv, gr_send, gr_recv, u_send, u_recv, near,
):
    row, col, rep = lax.axis_index("row"), lax.axis_index("col"), lax.axis_index("rep")
    y, x, core = row // 4, (row // 2) % 2, row % 2

    def at_row(yy, xx, cc):
        return lax.rem(yy + 4, 4) * 4 + xx * 2 + cc

    def wrap(v):
        return lax.rem(v + RING, RING)

    def place_of(dy, dx):
        return dy + dy // 2 - 2 * (dy // 3) + 4 * dx

    def remote(src, dst, ssem, rsem, where):
        return pltpu.make_async_remote_copy(
            src_ref=src, dst_ref=dst, send_sem=ssem, recv_sem=rsem,
            device_id=where, device_id_type=MESH,
        )

    here = (row, col, 1 - rep)
    sends = []

    def send(src, dst, ssem, rsem, where):
        copy = remote(src, dst, ssem, rsem, where)
        copy.start()
        sends.append(copy)

    def arrived(dst, rsem):
        remote(dst, dst, rsem, rsem, here).wait_recv()

    def sent(src, ssem):
        remote(src, src, ssem, ssem, here).wait_send()

    own_g = pltpu.make_async_copy(g_ref, gg.at[pl.ds(0, 2)], loc_sem.at[0])
    own_b = pltpu.make_async_copy(bt_ref, bt, loc_sem.at[1])
    own_x = pltpu.make_async_copy(x_ref, xg.at[pl.ds(PARTS * col, PARTS)], loc_sem.at[2])
    own_e = pltpu.make_async_copy(e_ref.at[0], e_in, loc_sem.at[3])
    for copy in (own_g, own_b, own_x, own_e):
        copy.start()

    barrier = pltpu.get_barrier_semaphore()

    def signal(where):
        pl.semaphore_signal(barrier, inc=1, device_id=where, device_id_type=MESH)

    right, left = (row, wrap(col + 1), rep), (row, wrap(col - 1), rep)
    up, down, side, sib = (
        (at_row(y + 1, x, core), col, rep),
        (at_row(y - 1, x, core), col, rep),
        (at_row(y, 1 - x, core), col, rep),
        (at_row(y, x, 1 - core), col, rep),
    )
    for where in (right, left, up, down, side, sib, here):
        signal(where)
    for k in (2, 3):
        signal((row, wrap(col + k), rep))
        signal((row, wrap(col - k), rep))

    def tell(k, *to):
        for where in to:
            pl.semaphore_signal(near.at[k], inc=1, device_id=where, device_id_type=MESH)

    def told(k, count):
        pl.semaphore_wait(near.at[k], count)

    own_g.wait()
    own_b.wait()
    quarter, group = lax.rem(col, 4), col // 4
    s_one[quarter] = dot(bt[...], gg[0:2].reshape(128, 1536), ((1,), (1,))).astype(BF16)
    own_x.wait()

    pl.semaphore_wait(barrier, 11)
    plane = (up, down, side, sib)

    def x_part(owner, part):
        return xg.at[PARTS * owner + part]

    def x_push(owner, part, k, side):
        ref = x_part(owner, part)
        recv = (xr_recv if side == 0 else xl_recv).at[PARTS * k + part]
        remote(ref, ref, x_send.at[side], recv, right if side == 0 else left).start()

    def x_turn(owner):
        slot = 2 * place_of(lax.rem(owner // 4 - y + 4, 4), lax.rem(owner // 2 + x, 2)) + lax.rem(owner + core, 2)
        xt[:, pl.ds(pl.multiple_of(slot * 128, 128), 128)] = xg[pl.ds(PARTS * owner, PARTS)].reshape(128, 384).T

    def x_step(k):
        frm, to = wrap(col - k), wrap(col + k)
        for i in range(PARTS):
            if k < 8 or i < PARTS // 2:
                arrived(x_part(frm, i), xr_recv.at[PARTS * (k - 1) + i])
                if k < 7 or (k == 7 and i < PARTS // 2):
                    x_push(frm, i, k, 0)
            i = PARTS - 1 - i
            if k < 8 or i >= PARTS // 2:
                arrived(x_part(to, i), xl_recv.at[PARTS * (k - 1) + i])
                if k < 7 or (k == 7 and i >= PARTS // 2):
                    x_push(to, i, k, 1)
        if k < 7:
            x_turn(frm)
            x_turn(to)

    OWN, YP, YM, Y2, XP, YPX, YMX, Y2X = range(8)
    FIRST, SECOND, WHOLE = (0, 1), (1, 1), (0, 2)

    def block(name, part, other=0):
        return gg.at[pl.ds(2 * (2 * name + other) + part[0], part[1])]

    def push(src, k, dst, where, part=WHOLE):
        remote(block(src, part), block(dst, part), g_send, g_recv.at[k], where).start()

    def got(k, name, part=WHOLE):
        arrived(block(name, part), g_recv.at[k])
        share(k, name, part)

    def share(k, name, part=WHOLE):
        remote(block(name, part), block(name, part, 1), d_send, d_recv.at[k], sib).start()

    def shared(k, name, part=WHOLE):
        arrived(block(name, part, 1), d_recv.at[k])

    def start_x():
        for part in range(PARTS):
            x_push(col, part, 0, 0)
            x_push(col, PARTS - 1 - part, 0, 1)
        x_turn(col)

    def start_g():
        push(OWN, 0, XP, side)
        push(OWN, 1, YM, up)
        push(OWN, 2, YP, down)
        share(9, OWN)

    def g_ym():
        got(1, YM)
        push(YM, 3, Y2, up, FIRST)

    def g_yp():
        got(2, YP)
        push(YP, 4, Y2, down, SECOND)

    def g_xp():
        got(0, XP)

    def p_xp():
        push(XP, 5, YMX, up)
        push(XP, 6, YPX, down)

    def g_y2():
        got(3, Y2, FIRST)
        push(Y2, 7, Y2X, side, FIRST)
        got(4, Y2, SECOND)
        push(Y2, 8, Y2X, side, SECOND)

    f_owner = quarter > 0
    f_count = 12

    def f_make():
        own_e.wait()
        ft = dot(bt[...], e_in[...], ((1,), (1,))).astype(BF16)
        for a in range(4):
            for b in range(3):
                f_out[4 * a + b + 1] = ft[16 * a:16 * a + 16, 128 * b:128 * b + 128]

    def f_send_out():
        @pl.loop(1, RING)
        def _(k):
            to = wrap(col + k)

            @pl.when(lax.rem(to, 4) > 0)
            def _():
                remote(f_out.at[to], f_in.at[col], f_send.at[0], f_recv.at[0], (row, to, rep)).start()

    def f_sum():
        @pl.when(f_owner)
        def _():
            f_in[col] = f_out[col]
            arrived(f_in.at[pl.ds(0, RING - 1)], f_recv.at[0])
            f_own[...] = jnp.sum(f_in[...].astype(F32), axis=0).astype(BF16)

            @pl.loop(1, RING)
            def _(k):
                remote(f_own, f_all.at[col], f_send.at[1], f_recv.at[1], (row, wrap(col + k), rep)).start()

            f_all[col] = f_own[...]
            sent(f_out.at[pl.ds(0, f_count - 1)], f_send.at[0])

    def f_end():
        @pl.when(f_owner)
        def _():
            arrived(f_all.at[pl.ds(0, f_count - 1)], f_recv.at[1])
            sent(f_in.at[pl.ds(0, RING - 1)], f_send.at[1])

        @pl.when(jnp.logical_not(f_owner))
        def _():
            arrived(f_all.at[pl.ds(0, f_count)], f_recv.at[1])
            sent(f_out.at[pl.ds(0, f_count)], f_send.at[0])

    def s_near():
        for k in range(1, 4):
            to = lax.rem(quarter + k, 4)
            send(s_one.at[quarter], s_one.at[quarter], s_send.at[0, k], s_recv.at[0, k], (row, group * 4 + to, rep))

    def s_far():
        for k in range(1, 4):
            arrived(s_one.at[lax.rem(quarter + 4 - k, 4)], s_recv.at[0, k])
        s_two[group] = jnp.sum(s_one[...].astype(F32), axis=0).astype(BF16)
        for k in range(1, 4):
            to = lax.rem(group + k, 4)
            send(s_two.at[group], s_two.at[group], s_send.at[1, k], s_recv.at[1, k], (row, to * 4 + quarter, rep))

    def s_row():
        for k in range(1, 4):
            arrived(s_two.at[lax.rem(group + 4 - k, 4)], s_recv.at[1, k])
        s_all[row] = jnp.sum(s_two[...].astype(F32), axis=0).astype(BF16)

        @pl.loop(1, RING)
        def _(k):
            remote(s_all.at[row], s_all.at[row], r_send.at[0], r_recv.at[0], (wrap(row + k), col, rep)).start()

    def s_end():
        arrived(s_all.at[pl.ds(0, RING - 1)], r_recv.at[0])

    def p_make():
        s_wide = jnp.concatenate([s_all[t] for t in range(RING)], axis=1)
        f_wide = jnp.concatenate(
            [jnp.concatenate([f_all[4 * a + b + 1] for a in range(4)], axis=0) for b in range(3)],
            axis=1,
        )
        p_part = dot(s_wide, xg[...].reshape(RING * 128, 384), ((1,), (0,)))
        p_mine[...] = (p_part + f_wide.astype(F32)).astype(BF16)
        send(p_mine, p_peer, p_send, p_recv, (row, col, 1 - rep))

    def multiply(first, count, base, out):
        ks = slice(256 * first, 256 * (first + count))

        @pl.loop(0, 3)
        def _(n):
            cols = pl.ds(pl.multiple_of(n * 512, 512), 512)
            gs = gg[4 * first:4 * (first + count), :, cols].reshape(256 * count, 512)
            out[:, cols] = (base[:, cols].astype(F32) + dot(xt[:, ks], gs, ((1,), (0,)))).astype(out.dtype)

    def c_one():
        shared(9, OWN)
        shared(1, YM)
        shared(2, YP)
        multiply(OWN, 3, e_in, acc)

    def c_two():
        shared(0, XP)
        shared(3, Y2, FIRST)
        shared(4, Y2, SECOND)
        multiply(Y2, 2, acc, acc)

    def g_rest():
        got(5, YMX)
        got(6, YPX)

    def g_last():
        got(7, Y2X, FIRST)
        got(8, Y2X, SECOND)

    def c_three():
        shared(5, YMX)
        shared(6, YPX)
        multiply(YPX, 2, acc, acc)

    def c_four():
        shared(7, Y2X, FIRST)
        shared(8, Y2X, SECOND)
        multiply(Y2X, 1, acc, comp_ref)

    def t_zero():
        tell(0, right, left)
        tell(3, *plane)

    def t_one():
        told(0, 2)
        tell(1, (row, wrap(col + 4), rep), (row, wrap(col - 4), rep))
        told(3, 4)
        tell(4, *plane)

    def t_three():
        told(1, 2)
        told(4, 4)
        tell(5, *plane)

    def t_four():
        told(5, 4)
        tell(6, here)

    def t_five():
        told(6, 1)

    s_near()
    start_x()
    start_g()
    t_zero()
    f_make()
    t_one()
    x_step(1)
    t_three()
    s_far()
    x_step(2)
    f_send_out()
    t_four()
    x_step(3)
    g_ym()
    g_yp()
    g_xp()
    p_xp()
    x_step(4)
    f_sum()
    s_row()
    x_step(5)
    g_y2()
    x_step(6)
    f_end()
    x_step(7)
    g_rest()
    s_end()
    x_step(8)
    p_make()
    for k in (7, 8, 9):
        x_turn(wrap(col + k))
    g_last()
    c_one()
    c_two()
    t_five()
    c_three()
    c_four()
    arrived(p_peer, p_recv)
    p_t = (p_mine[...].astype(F32) + p_peer[...].astype(F32)) * 0.5

    comp_out = pltpu.make_async_copy(comp_ref, comp_hbm, loc_sem.at[0])
    comp_out.start()

    p_high = p_t.astype(BF16)
    p_rest = (p_t - p_high.astype(F32)).astype(BF16)
    p_both = jnp.concatenate([p_high, p_rest], axis=0)
    me = row + RING * rep
    mine = row // 2 + 8 * rep
    owner = core == x

    def piece_at(k):
        chip = lax.rem(k, 8)
        return (2 * chip + lax.rem(chip, 2), col, k // 8)

    for b in range(4):
        cols = slice(384 * b, 384 * b + 384)
        ut = dot(p_both, comp_ref[:, cols], ((1,), (0,)))
        ut = (ut[:RANK] + ut[RANK:]).astype(BF16)
        for a in range(4):
            u_out[4 * a + b] = ut[16 * a:16 * a + 16, :]

    @pl.loop(0, RING)
    def _(k):
        @pl.when(jnp.logical_not(jnp.logical_and(owner, k == mine)))
        def _():
            remote(u_out.at[k], u_in.at[me], u_send.at[0], u_recv.at[0], piece_at(k)).start()

    gram = dot(p_t, p_t, ((1,), (1,)), HIGH)
    gram_mine[...] = jnp.concatenate([gram[:32], gram[32:]], axis=1)

    @pl.loop(1, RING)
    def _(k):
        to = wrap(row + k)
        remote(gram_mine, gram_all.at[row], gr_send, gr_recv, (to, col, rep)).start()

    gram_all[row] = gram_mine[...]

    @pl.when(owner)
    def _():
        u_in[me] = u_out[mine]
        arrived(u_in.at[pl.ds(0, 31)], u_recv.at[0])
        u_own[...] = jnp.sum(u_in[...].astype(F32), axis=0).astype(BF16)

        for dy in (2, 3, 1, 0):
            base = lax.rem(y + dy, 4) * 4

            @pl.loop(0, 8)
            def _(k):
                to = base + lax.rem(k, 4)

                def go():
                    remote(u_own, u_all.at[mine], u_send.at[1], u_recv.at[1], (to, col, k // 4)).start()

                if dy:
                    go()
                else:
                    pl.when(to + RING * (k // 4) != me)(go)

        u_all[mine] = u_own[...]

    arrived(gram_all.at[pl.ds(0, RING - 1)], gr_recv)
    total = jnp.sum(gram_all[...], axis=0)
    gram = jnp.concatenate([total[:, :RANK], total[:, RANK:]], axis=0)
    subl = lax.broadcasted_iota(jnp.int32, (RANK, 128), 0)
    lane = lax.broadcasted_iota(jnp.int32, (RANK, 128), 1)
    mat[...] = jnp.concatenate([gram, (subl == lane)[:, :RANK].astype(F32)], axis=1)

    def pick(rows, k):
        return jnp.sum(jnp.where(lane[:rows.shape[0]] == k, rows, 0.0), axis=1, keepdims=True)

    def eliminate(h, carry):
        k = 2 * h
        m = mat[...]
        row_a, row_b = mat[pl.ds(k, 1), :], mat[pl.ds(k + 1, 1), :]
        col_a, col_b = pick(m, k), pick(m, k + 1)
        corner, cross = pick(row_a, k), pick(row_a, k + 1)
        below, last = pick(row_b, k), pick(row_b, k + 1)
        inverse = 1.0 / corner
        step = below * inverse
        row_b = row_b - step * row_a
        factor_a = col_a * inverse
        factor_b = (col_b - factor_a * cross) / (last - step * cross)
        factor_a = jnp.where(subl[:, :1] > k, factor_a, 0.0)
        factor_b = jnp.where(subl[:, :1] > k + 1, factor_b, 0.0)
        mat[...] = m - factor_a * row_a - factor_b * row_b
        return carry

    lax.fori_loop(0, RANK // 2, eliminate, 0)
    d = jnp.sum(jnp.where(lane == subl, mat[...], 0.0), axis=1, keepdims=True)
    inv_factor = lax.rsqrt(d) * mat[:, RANK:]
    ortho_ref[...] = dot(inv_factor, p_t, ((1,), (0,)), HIGH).astype(BF16)

    @pl.when(owner)
    def _():
        arrived(u_all.at[pl.ds(0, 15)], u_recv.at[1])
        sent(u_out.at[pl.ds(0, 15)], u_send.at[0])
        sent(u_in.at[pl.ds(0, 31)], u_send.at[1])

    @pl.when(jnp.logical_not(owner))
    def _():
        arrived(u_all, u_recv.at[1])
        sent(u_out, u_send.at[0])

    for b in range(4):
        ut = jnp.concatenate([u_all[4 * a + b] for a in range(4)], axis=0).astype(F32) * 0.5
        basis_ref[:, 384 * b:384 * b + 384] = dot(inv_factor, ut, ((1,), (0,)), HIGH)

    comp_out.wait()
    for copy in sends:
        copy.wait_send()
    for k in range(2):
        sent(xg.at[pl.ds(0, 7 * PARTS + PARTS // 2)], x_send.at[k])
    sent(gg.at[pl.ds(0, 14)], g_send)
    sent(gg.at[pl.ds(0, 16)], d_send)
    sent(s_all.at[pl.ds(0, 15)], r_send.at[0])
    sent(gram_all.at[pl.ds(0, 15)], gr_send)


def body(layer_inputs, output_grads, error_prev, basis_prev):
    dma = pltpu.SemaphoreType.DMA
    vmem = pltpu.VMEM
    comp, ortho_t, basis_t = pl.pallas_call(
        kernel,
        out_shape=(
            jax.ShapeDtypeStruct((384, 1536), BF16),
            jax.ShapeDtypeStruct((RANK, 384), BF16),
            jax.ShapeDtypeStruct((RANK, 1536), F32),
        ),
        in_specs=[pl.BlockSpec(memory_space=pl.ANY)] * 4,
        out_specs=[pl.BlockSpec(memory_space=pl.ANY)] + [pl.BlockSpec(memory_space=vmem)] * 2,
        scratch_shapes=[
            vmem((16 * PARTS, ROWS, 384), BF16),
            vmem((32, HALF, 1536), BF16),
            vmem((384, 1536), F32),
            vmem((384, 2048), BF16),
            vmem((384, 1536), BF16),
            vmem((384, 1536), BF16),
            vmem((RANK, 1536), BF16),
            vmem((4, RANK, 128), BF16),
            vmem((4, RANK, 128), BF16),
            vmem((16, 16, 128), BF16),
            vmem((16, 16, 128), BF16),
            vmem((16, 128), BF16),
            vmem((16, 16, 128), BF16),
            vmem((16, RANK, 128), BF16),
            vmem((RANK, 384), BF16),
            vmem((RANK, 384), BF16),
            vmem((32, 128), F32),
            vmem((16, 32, 128), F32),
            vmem((RANK, 128), F32),
            vmem((16, 16, 384), BF16),
            vmem((32, 16, 384), BF16),
            vmem((16, 384), BF16),
            vmem((16, 16, 384), BF16),
            dma((4,)),
            dma((2,)), dma((8 * PARTS,)), dma((8 * PARTS,)),
            dma(()), dma((9,)), dma(()), dma((10,)),
            dma((2, 4)), dma((2, 4)), dma((2,)), dma((2,)), dma((1,)), dma((1,)),
            dma(()), dma(()), dma(()), dma(()), dma((2,)), dma((2,)),
            pltpu.SemaphoreType.REGULAR((7,)),
        ],
        compiler_params=pltpu.CompilerParams(
            collective_id=0, has_side_effects=True, vmem_limit_bytes=60 * 2**20
        ),
        name="powersgd",
    )(layer_inputs.reshape(PARTS, ROWS, 384), output_grads.reshape(2, HALF, 1536), error_prev, basis_prev.T)
    basis_next = basis_t.T
    approx = dot(ortho_t, basis_t.astype(BF16), ((0,), (0,)))
    error_next = (comp.astype(F32) - approx).astype(BF16)
    return (basis_next, error_next[None])


def solution(mesh):
    return jax.shard_map(
        body,
        mesh=mesh,
        in_specs=(
            P("rep", "col", "row"),
            P("rep", "row", "col"),
            P("rep", "row", "col"),
            P("col", None),
        ),
        out_specs=(P("col", None), P("rep", "row", "col")),
        check_vma=False,
    )
```
